128 devices in a mesh: row: 4 (over x), col: 16 (over z, y), depth: 2 (over core).
Axes of the slice: x: 4, y: 4, z: 4, core: 2. Of those that a mesh axis runs over, the one named last changes fastest.
Arguments:
- density: float32 [4096, 4096], P('row', 'col'), as said below
- pattern: int32 [64, 64], P('row', 'col'), may hold values from 0 to 1, as said below
- branches: int32 [3], replicated, may hold values from 0 to 1, as said below
Outputs:
- purified: float32 [4096, 4096], P('row', 'col')
- traces: float32 [3], replicated
The draws below stay inside these ranges and needn't reach their ends.
Inputs may be any that keep to these rules, and one draw needn't show every extreme that they name: `pattern`: symmetric, and every diagonal block is 1. `density`: symmetric, and zero in every block where pattern is 0. `branches`: the first step's value differs from the last step's.
All inputs are finite; a program needn't handle non-finite values.
Results may differ from the reference program's by a relative error of at most 0.00015.
Values sent between devices are 32-bit elements; how exact they have to be, the bound alone decides.
A program may use at most 64 MiB of HBM per device.

```python
import jax
import jax.numpy as jnp
from jax import lax

BS = 64
STEPS = 3
NB = 64
M = 4096


def block_pattern(key):
    scores = jax.random.randint(key, (NB, NB), 0, NB)
    lowest = jnp.minimum(scores, scores.T)
    index = jnp.arange(NB)
    distance = jnp.abs(index[:, None] - index[None, :])
    kept = (100 * lowest + 42 * distance < 45 * NB) | (distance == 0)
    return jnp.where(kept, 1, 0).astype(jnp.int32)


def draw_pattern(key, part):
    return block_pattern(key)


def draw_branches(key, part):
    key = jax.random.fold_in(key, 11)
    picks = jax.random.randint(key, (STEPS,), 0, 2).astype(jnp.int32)
    return picks.at[0].set(1 - picks[STEPS - 1])


def draw_density(key, part):
    chosen = block_pattern(key)
    key = jax.random.fold_in(key, 7)
    first_key, second_key = jax.random.split(key)
    noise = jax.random.normal(first_key, (M, M), jnp.float32)
    factor = jax.random.uniform(second_key, (M,), jnp.float32, 0.7, 1.3)
    symmetric = (noise + noise.T) * 0.7071
    spread = 0.15 * (BS * (1.0 + NB * 0.5)) ** (-0.5)
    keep = jnp.repeat(jnp.repeat(chosen.astype(jnp.float32), BS, axis=0), BS, axis=1)
    position = jnp.arange(M, dtype=jnp.float32)
    diagonal = (0.25 + 0.5 * position / M) * factor
    identity = (jnp.arange(M)[:, None] == jnp.arange(M)[None, :]).astype(jnp.float32)
    return keep * symmetric * spread + identity * diagonal[None, :]


def setup_inputs(seed: int = 0) -> dict:
    key_list = jax.random.split(jax.random.key(seed), 4)
    return {
        "density": draw_density(jax.random.fold_in(key_list[3], 71), 0),
        "pattern": draw_pattern(jax.random.fold_in(key_list[3], 71), 0),
        "branches": draw_branches(jax.random.fold_in(key_list[3], 71), 0),
    }


def reference(density, pattern, branches):
    keep = jnp.repeat(jnp.repeat(pattern.astype(jnp.float32), BS, axis=0), BS, axis=1)
    current = density
    collected = []
    for section in range(STEPS):
        square = jnp.dot(current, current, precision=lax.Precision.HIGHEST, preferred_element_type=jnp.float32)
        collected.append(jnp.trace(square))
        weight = branches[section].astype(jnp.float32)
        current = keep * (square + 2.0 * weight * (current - square))
    return current, jnp.stack(collected)
```

```python
import functools

import jax
import jax.numpy as jnp
from jax import lax
from jax.experimental import pallas as pl
from jax.experimental.pallas import tpu as pltpu
from jax.sharding import PartitionSpec as P

MESH = pl.DeviceIdType.MESH
STEPS = 3
BS = 64
BLK = 1024
SLAB = 128
CH = 32
ROLES = (("x", "z", "y"), ("z", "y", "x"), ("y", "x", "z"))
PLUS_ORDER = (0, 1, 2, 3)
MINUS_ORDER = (2, 3, 0, 1)
F32 = jnp.float32
BF16 = jnp.bfloat16


def nt_dot(left, right):
    return lax.dot_general(left, right, (((1,), (1,)), ((), ())), preferred_element_type=F32)


def split(value):
    high = value.astype(BF16)
    return high, (value - high.astype(F32)).astype(BF16)


def body(
    dens, pat, br, out, tr_out,
    pbuf, qbuf, phi, plo, qhi, qlo, obuf, r1, r2, patf, gbuf, vsend, vcore, vaxis, fin,
    ag_s, ag_r, cx_s, cx_r, bc_s, bc_r, rs_s, rs_r, pt_s, pt_r, tr_s, tr_r, fx_s, fx_r,
):
    col = lax.axis_index("col")
    k = lax.axis_index("depth")
    pos = {"x": lax.axis_index("row"), "y": lax.rem(col, 4), "z": lax.div(col, 4)}
    other = 1 - k

    def wrap(value):
        return lax.rem(value + 8, 4)

    def device(x, y, z, core):
        return (x, z * 4 + y, core)

    def at(axis, delta):
        place = dict(pos)
        place[axis] = wrap(place[axis] + delta)
        return device(place["x"], place["y"], place["z"], k)

    partner = device(pos["x"], pos["y"], pos["z"], other)

    def rcopy(src, dst, send, recv, dev):
        return pltpu.make_async_remote_copy(
            src_ref=src, dst_ref=dst, send_sem=send, recv_sem=recv, device_id=dev, device_id_type=MESH
        )

    own0 = pos["y"] * 2 + k
    for i in range(8):
        piece = dens[i * 128:(i + 1) * 128, pl.ds(pl.multiple_of(k * 128, 128), 128)]
        pbuf[0, own0, :, i * 128:(i + 1) * 128] = piece.T
    patf[...] = jnp.zeros_like(patf)
    vsend[0] = jnp.zeros((8, 128), F32)
    patf[:, 0:4] = pat[...].astype(F32)

    barrier = pltpu.get_barrier_semaphore()
    greet = [partner]
    for axis in ("x", "y", "z"):
        for delta in (1, -1, 2):
            greet.append(at(axis, delta))
    for i in range(4):
        greet.append(device(pos["y"], i, pos["z"], other))
        greet.append(device(pos["x"], i, pos["y"], other))
    for dev in greet:
        pl.semaphore_signal(barrier, inc=1, device_id=dev, device_id_type=MESH)
    pl.semaphore_wait(barrier, len(greet))

    def pattern_copies():
        found = []
        for i in range(4):
            found.append(rcopy(patf, gbuf.at[0, pos["y"]], pt_s.at[0, i], pt_r.at[0, pos["y"]],
                               device(i, pos["x"], pos["z"], other)))
            found.append(rcopy(patf, gbuf.at[1, pos["y"]], pt_s.at[1, i], pt_r.at[1, pos["y"]],
                               device(pos["x"], pos["z"], i, other)))
        return found

    def pattern_wait(s):
        for i in range(4):
            rcopy(patf, gbuf.at[s, i], pt_s.at[s, i], pt_r.at[s, i], partner).wait_recv()

    def square_sum(s, slab):
        total = jnp.zeros((1, BLK), F32)
        for i in range(4):
            part = pbuf[s, slab, i * 32:(i + 1) * 32, :]
            total = total + jnp.sum(part * part, axis=0, keepdims=True)
        vsend[0, s:s + 1, :] = jnp.broadcast_to(jnp.sum(total, axis=1, keepdims=True), (1, 128))

    def trace_core_start():
        rcopy(vsend.at[0], vcore, tr_s.at[0, 0], tr_r.at[0, 0], partner).start()

    def trace_core_end():
        copy = rcopy(vsend.at[0], vcore, tr_s.at[0, 0], tr_r.at[0, 0], partner)
        copy.wait_recv()
        copy.wait_send()
        vsend[1] = vsend[0] + vcore[...]

    def trace_axis_copies(stage, axis):
        me = pos[axis]
        return [
            rcopy(vsend.at[stage], vaxis.at[stage, me], tr_s.at[stage, d], tr_r.at[stage, me], at(axis, d))
            for d in (1, 2, 3)
        ]

    def trace_axis_start(stage, axis):
        for copy in trace_axis_copies(stage, axis):
            copy.start()
        vaxis[stage, pos[axis]] = vsend[stage]

    def trace_axis_end(stage, axis):
        for d in (1, 2, 3):
            src = wrap(pos[axis] + d)
            rcopy(vsend.at[stage], vaxis.at[stage, src], tr_s.at[stage, d], tr_r.at[stage, src], partner).wait_recv()
        for copy in trace_axis_copies(stage, axis):
            copy.wait_send()
        vsend[stage + 1] = (vaxis[stage, 0] + vaxis[stage, 1]) + (vaxis[stage, 2] + vaxis[stage, 3])

    for s in range(STEPS):
        an, bn, cn = ROLES[s]
        a, b, c = pos[an], pos[bn], pos[cn]
        d = wrap(b - c)
        root = d == 0
        own = c * 2 + k

        def rows(j):
            return pl.ds(j * CH, CH)

        def ag_copy(direction, i):
            sign = 1 if direction == 0 else -1
            order = PLUS_ORDER if direction == 0 else MINUS_ORDER
            if i < 4:
                slab, chunk = own, order[i]
            else:
                slab, chunk = wrap(c - sign) * 2 + k, order[i - 4]
            ref = pbuf.at[s, slab, rows(chunk)]
            return rcopy(ref, ref, ag_s.at[s, direction, i], ag_r.at[s, direction, i], at(cn, sign))

        def ag_arrival(direction, i):
            sign = 1 if direction == 0 else -1
            order = PLUS_ORDER if direction == 0 else MINUS_ORDER
            if i < 4:
                return wrap(c - sign), order[i]
            return wrap(c + 2), order[i - 4]

        def ag_wait(direction, i):
            q, chunk = ag_arrival(direction, i)
            ref = pbuf.at[s, q * 2 + k, rows(chunk)]
            rcopy(ref, ref, ag_s.at[s, direction, i], ag_r.at[s, direction, i], partner).wait_recv()

        def cx_copy(i):
            if i == 0:
                ref = pbuf.at[s, own]
            else:
                q, chunk = ag_arrival((i - 1) % 2, (i - 1) // 2)
                ref = pbuf.at[s, q * 2 + k, rows(chunk)]
            return rcopy(ref, ref, cx_s.at[s, i], cx_r.at[s, i], partner)

        def cx_wait(i):
            if i == 0:
                ref = pbuf.at[s, c * 2 + other]
            else:
                q, chunk = ag_arrival((i - 1) % 2, (i - 1) // 2)
                ref = pbuf.at[s, q * 2 + other, rows(chunk)]
            rcopy(ref, ref, cx_s.at[s, i], cx_r.at[s, i], partner).wait_recv()

        def bc_place(direction, seq):
            half = lax.div(seq, 2)
            near = -1 if direction == 0 else 1
            offset = jnp.where(half == 0, 0, jnp.where(half == 1, near, jnp.where(half == 2, -near, 2)))
            chunk = lax.rem(seq, 2) + (0 if direction == 0 else 2)
            return wrap(c + offset), pl.multiple_of(chunk * CH, CH)

        def bc_copy(direction, seq, from_root):
            q, row = bc_place(direction, seq)
            dst = qbuf.at[s, q, pl.ds(row, CH)]
            src = pbuf.at[s, q * 2 + k, pl.ds(row, CH)] if from_root else dst
            return rcopy(src, dst, bc_s.at[s, direction, seq], bc_r.at[s, direction, seq],
                         at(bn, 1 if direction == 0 else -1))

        for i in range(4):
            ag_copy(0, i).start()
            ag_copy(1, i).start()
        cx_copy(0).start()

        @pl.when(root)
        def _():
            for seq in range(2):
                bc_copy(0, jnp.int32(seq), True).start()
                bc_copy(1, jnp.int32(seq), True).start()

        if s == 0:
            for copy in pattern_copies():
                copy.start()
        square_sum(s, own)
        if s == 2:
            trace_core_start()

        for tick in range(10):
            if tick < 6:
                for direction in (0, 1):
                    ag_wait(direction, tick)
                    if tick < 2:
                        ag_copy(direction, tick + 4).start()
                for direction in (0, 1):
                    cx_copy(1 + 2 * tick + direction).start()

                @pl.when(root)
                def _():
                    bc_copy(0, jnp.int32(tick + 2), True).start()
                    bc_copy(1, jnp.int32(tick + 2), True).start()

            for direction in (0, 1):
                lag = d - 1 if direction == 0 else 3 - d
                seq = tick - lag

                @pl.when(jnp.logical_and(d > 0, jnp.logical_and(seq >= 0, seq < 8)))
                def _():
                    copy = bc_copy(direction, seq, False)
                    copy.wait_recv()

                    @pl.when(lag < 2)
                    def _():
                        copy.start()

        for i in range(13):
            cx_wait(i)
        if s == 2:
            trace_core_end()
            trace_axis_start(1, "x")

        @pl.loop(0, 8)
        def _(j):
            row = pl.multiple_of(j * SLAB, SLAB)
            high, low = split(pbuf[s, j])
            phi[pl.ds(row, SLAB), :] = high
            plo[pl.ds(row, SLAB), :] = low

        @pl.when(root)
        def _():
            @pl.loop(0, 4)
            def _(q):
                row = pl.multiple_of(q * SLAB, SLAB)
                high, low = split(pbuf[s, q * 2 + k])
                qhi[pl.ds(row, SLAB), :] = high
                qlo[pl.ds(row, SLAB), :] = low

        @pl.when(jnp.logical_not(root))
        def _():
            @pl.loop(0, 4)
            def _(q):
                row = pl.multiple_of(q * SLAB, SLAB)
                high, low = split(qbuf[s, q])
                qhi[pl.ds(row, SLAB), :] = high
                qlo[pl.ds(row, SLAB), :] = low

        weight = br[s].astype(F32)
        scale = 1.0 - 2.0 * weight
        linear = 2.0 * weight * (a == b).astype(F32)

        @pl.loop(0, 4)
        def _(n):
            at_col = pl.multiple_of(n * 256, 256)
            high = phi[pl.ds(at_col, 256), :]
            low = plo[pl.ds(at_col, 256), :]
            value = nt_dot(qhi[...], high) + nt_dot(qhi[...], low) + nt_dot(qlo[...], high)
            same = qhi[:, pl.ds(at_col, 256)].astype(F32) + qlo[:, pl.ds(at_col, 256)].astype(F32)
            obuf[:, pl.ds(at_col, 256)] = scale * value + linear * same

        def slab_rows(q, first, count):
            return pl.ds(pl.multiple_of(q * SLAB + first, 64), count)

        up, down, far = wrap(a + 1), wrap(a - 1), wrap(a + 2)

        def rs_copy(direction, i):
            sign = 1 if direction == 0 else -1
            near = up if direction == 0 else down
            first = 0 if direction == 0 else 64
            if i == 0:
                src, dst = obuf.at[slab_rows(far, first, 64)], r1.at[s, direction]
            elif i == 1:
                src, dst = obuf.at[slab_rows(near, 64 - first, 64)], r2.at[s, direction, pl.ds(64 - first, 64)]
            else:
                src, dst = obuf.at[slab_rows(near, first, 64)], r2.at[s, direction, pl.ds(first, 64)]
            return rcopy(src, dst, rs_s.at[s, direction, i], rs_r.at[s, direction, i], at(an, sign))

        for i in (0, 1):
            for direction in (0, 1):
                rs_copy(direction, i).start()
        if s == 2:
            trace_axis_end(1, "x")
            trace_axis_start(2, "y")
        for direction in (0, 1):
            rs_copy(direction, 0).wait_recv()
            near = up if direction == 0 else down
            part = slab_rows(near, 0 if direction == 0 else 64, 64)
            obuf[part, :] = obuf[part, :] + r1[s, direction]
            rs_copy(direction, 2).start()
        if s == 2:
            trace_axis_end(2, "y")
            trace_axis_start(3, "z")

        if s < 2:
            pattern_wait(s)
            line = lax.broadcasted_iota(jnp.int32, (SLAB, 16), 0)
            block = lax.broadcasted_iota(jnp.int32, (SLAB, 16), 1)
            pick = (block == a * 4 + k * 2 + line // BS).astype(F32)
            left = lax.broadcasted_iota(jnp.int32, (128, 256), 0)
            right = lax.broadcasted_iota(jnp.int32, (128, 256), 1)
            spread = (left == right // BS).astype(F32)
        for i in (1, 2):
            for direction in (0, 1):
                rs_copy(direction, i).wait_recv()
        for i in range(4):
            lanes = slice(i * 256, (i + 1) * 256)
            value = obuf[slab_rows(a, 0, SLAB), lanes] + r2[s, 0, :, lanes] + r2[s, 1, :, lanes]
            if s < 2:
                chosen = jnp.dot(pick, gbuf[s, i], preferred_element_type=F32)
                pbuf[s + 1, a * 2 + k, :, lanes] = value * jnp.dot(chosen, spread, preferred_element_type=F32)
            else:
                fin[k, :, lanes] = value

        for direction in (0, 1):
            for i in range(6):
                ag_copy(direction, i).wait_send()
            for i in range(3):
                rs_copy(direction, i).wait_send()

            @pl.when(d != (3 if direction == 0 else 1))
            def _():
                for seq in range(8):
                    bc_copy(direction, jnp.int32(seq), False).wait_send()
        for i in range(13):
            cx_copy(i).wait_send()
        if s == 0:
            for copy in pattern_copies():
                copy.wait_send()

    last = rcopy(fin.at[k], fin.at[k], fx_s, fx_r, partner)
    last.start()
    trace_axis_end(3, "z")
    tr_out[...] = vsend[4]
    left = lax.broadcasted_iota(jnp.int32, (128, 256), 0)
    right = lax.broadcasted_iota(jnp.int32, (128, 256), 1)
    spread = (left == right // BS).astype(F32)
    line = lax.broadcasted_iota(jnp.int32, (128, 16), 0)
    block = lax.broadcasted_iota(jnp.int32, (128, 16), 1)
    rcopy(fin.at[other], fin.at[other], fx_s, fx_r, partner).wait_recv()
    for i in range(8):
        pick = (block == i * 2 + line // BS).astype(F32)
        chosen = jnp.dot(pick, patf[...], preferred_element_type=F32)
        mask = jnp.dot(chosen, spread, preferred_element_type=F32)
        for half in range(2):
            lanes = slice(half * 128, (half + 1) * 128)
            part = fin[half, :, i * 128:(i + 1) * 128].T
            out[i * 128:(i + 1) * 128, lanes] = part * mask[:, lanes]
    last.wait_send()


def per_device(density, pattern, branches):
    vmem = pl.BlockSpec(memory_space=pltpu.VMEM)
    dma = pltpu.SemaphoreType.DMA
    purified, traces = pl.pallas_call(
        body,
        out_shape=(
            jax.ShapeDtypeStruct((BLK, 256), F32),
            jax.ShapeDtypeStruct((8, 128), F32),
        ),
        in_specs=[vmem, vmem, pl.BlockSpec(memory_space=pltpu.SMEM)],
        out_specs=(vmem, vmem),
        scratch_shapes=[
            pltpu.VMEM((STEPS, 8, SLAB, BLK), F32),
            pltpu.VMEM((STEPS, 4, SLAB, BLK), F32),
            pltpu.VMEM((BLK, BLK), BF16),
            pltpu.VMEM((BLK, BLK), BF16),
            pltpu.VMEM((512, BLK), BF16),
            pltpu.VMEM((512, BLK), BF16),
            pltpu.VMEM((512, BLK), F32),
            pltpu.VMEM((STEPS, 2, 64, BLK), F32),
            pltpu.VMEM((STEPS, 2, SLAB, BLK), F32),
            pltpu.VMEM((16, 128), F32),
            pltpu.VMEM((2, 4, 16, 128), F32),
            pltpu.VMEM((5, 8, 128), F32),
            pltpu.VMEM((8, 128), F32),
            pltpu.VMEM((4, 4, 8, 128), F32),
            pltpu.VMEM((2, SLAB, BLK), F32),
            dma((STEPS, 2, 6)), dma((STEPS, 2, 6)),
            dma((STEPS, 13)), dma((STEPS, 13)),
            dma((STEPS, 2, 8)), dma((STEPS, 2, 8)),
            dma((STEPS, 2, 3)), dma((STEPS, 2, 3)),
            dma((2, 4)), dma((2, 4)),
            dma((4, 4)), dma((4, 4)),
            dma, dma,
        ],
        compiler_params=pltpu.CompilerParams(
            collective_id=0, has_side_effects=True, vmem_limit_bytes=56 * 2**20
        ),
        name="purify",
    )(density, pattern, branches)
    return purified, traces[:STEPS, 0]


def solution(mesh):
    return jax.shard_map(
        per_device,
        mesh=mesh,
        in_specs=(P("row", "col"), P("row", "col"), P()),
        out_specs=(P("row", "col"), P()),
        check_vma=False,
    )
```

```python
import functools

import jax
import jax.numpy as jnp
from jax import lax
from jax.experimental import pallas as pl
from jax.experimental.pallas import tpu as pltpu
from jax.sharding import PartitionSpec as P

MESH = pl.DeviceIdType.MESH
STEPS = 3
BS = 64
BLK = 1024
SLAB = 128
CH = 32
HALF = 16
LAG = 3
OFFSETS = (0, -1, 1, 2)
START_AT = (0.0, 34.0, 72.0)
ARRIVE = (
    {
        "direct": (4.5, 7.4, 11.8, 16.2), "handed": (9.0, 13.3, 17.7, 19.2), "split_p": (11.0, 15.3, 19.7, 21.2),
        "sum": 1.0, "tick": lambda t: 3.0 + 4.5 * (t > 0) + 1.5 * t + 1.5 * (t > 2),
        "piece": (19.8, 25.0, 30.0, 36.0), "product": (21.3, 25.3, 31.0, 37.0),
        "add_on": (26.0, 29.8, 34.5, 39.7), "finish": (31.0, 35.0, 39.8, 43.0),
    },
    {
        "direct": (6.0, 9.6, 14.0, 19.0), "handed": (9.5, 14.1, 19.1, 24.0), "split_p": (11.5, 16.1, 21.1, 26.0),
        "sum": 12.5, "tick": lambda t: 3.5 + 4.0 * (t > 0) + 1.5 * t + 1.5 * (t > 2),
        "piece": (22.0, 28.0, 30.0, 36.0), "product": (26.1, 28.1, 31.5, 37.0),
        "add_on": (31.0, 34.0, 36.5, 41.0), "finish": (36.0, 39.0, 42.0, 46.0),
    },
)
ROLES = (("x", "z", "y"), ("z", "y", "x"), ("y", "x", "z"))
F32 = jnp.float32
BF16 = jnp.bfloat16


def nt_dot(left, right):
    return lax.dot_general(left, right, (((1,), (1,)), ((), ())), preferred_element_type=F32)


def split(value):
    high = value.astype(BF16)
    return high, (value - high.astype(F32)).astype(BF16)


def lane_rows(i):
    unit = i // 2
    return [(2 * (i % 2) + q) * 256 + core * SLAB + unit * CH for q in (0, 1) for core in (0, 1)]


def body(
    dens, pat, br, out, tr_out,
    pbuf, qbuf, phi, plo, qcat, obuf, r1, r2, patf, gbuf, mbuf, vsend, vcore, vaxis, fin,
    ag_s, ag_r, af_s, af_r, cx_s, cx_r, bc_s, bc_r, rs_s, rs_r, pt_s, pt_r, tr_s, tr_r, fx_s, fx_r,
):
    col = lax.axis_index("col")
    k = lax.axis_index("depth")
    pos = {"x": lax.axis_index("row"), "y": lax.rem(col, 4), "z": lax.div(col, 4)}
    other = 1 - k

    def wrap(value):
        return lax.rem(value + 8, 4)

    def device(x, y, z, core):
        return (x, z * 4 + y, core)

    def at(axis, delta):
        place = dict(pos)
        place[axis] = wrap(place[axis] + delta)
        return device(place["x"], place["y"], place["z"], k)

    partner = device(pos["x"], pos["y"], pos["z"], other)

    def rcopy(src, dst, send, recv, dev):
        return pltpu.make_async_remote_copy(
            src_ref=src, dst_ref=dst, send_sem=send, recv_sem=recv, device_id=dev, device_id_type=MESH
        )

    barrier = pltpu.get_barrier_semaphore()
    greet = [partner]
    for axis in ("x", "y", "z"):
        for delta in (1, -1, 2):
            greet.append(at(axis, delta))
    for i in range(4):
        greet.append(device(pos["y"], i, pos["z"], other))
        greet.append(device(pos["x"], i, pos["y"], other))
    for dev in greet:
        pl.semaphore_signal(barrier, inc=1, device_id=dev, device_id_type=MESH)

    for i in range(8):
        mine = pl.ds(pl.multiple_of(k * 128, 128), 128)
        piece = jnp.concatenate([dens[row:row + CH, mine] for row in lane_rows(i)], axis=0)
        pbuf[0, pos["y"], k, :, i * 128:(i + 1) * 128] = piece.T
    patf[...] = jnp.zeros_like(patf)
    vsend[0] = jnp.zeros((8, 128), F32)
    patf[:, 0:4] = pat[...].astype(F32)
    pl.semaphore_wait(barrier, len(greet))

    def pattern_copies():
        found = []
        for i in range(4):
            found.append(rcopy(patf, gbuf.at[0, pos["y"]], pt_s.at[0, i], pt_r.at[0, pos["y"]],
                               device(i, pos["x"], pos["z"], other)))
            found.append(rcopy(patf, gbuf.at[1, pos["y"]], pt_s.at[1, i], pt_r.at[1, pos["y"]],
                               device(pos["x"], pos["z"], i, other)))
        return found

    def pattern_wait(s):
        for i in range(4):
            rcopy(patf, gbuf.at[s, i], pt_s.at[s, i], pt_r.at[s, i], partner).wait_recv()

    def square_sum(s, slab):
        total = jnp.zeros((1, BLK), F32)
        for i in range(4):
            part = pbuf[s, slab, k, i * CH:(i + 1) * CH, :]
            total = total + jnp.sum(part * part, axis=0, keepdims=True)
        vsend[0, s:s + 1, :] = jnp.broadcast_to(jnp.sum(total, axis=1, keepdims=True), (1, 128))

    def trace_core():
        return rcopy(vsend.at[0], vcore, tr_s.at[0, 0], tr_r.at[0, 0], partner)

    def trace_core_end():
        trace_core().wait()
        vsend[1] = vsend[0] + vcore[...]

    def trace_axis_copies(stage, axis):
        me = pos[axis]
        return [
            rcopy(vsend.at[stage], vaxis.at[stage, me], tr_s.at[stage, d], tr_r.at[stage, me], at(axis, d))
            for d in (1, 2, 3)
        ]

    def trace_axis_start(stage, axis):
        for copy in trace_axis_copies(stage, axis):
            copy.start()
        vaxis[stage, pos[axis]] = vsend[stage]

    def trace_axis_end(stage, axis):
        for d in (1, 2, 3):
            src = wrap(pos[axis] + d)
            rcopy(vsend.at[stage], vaxis.at[stage, src], tr_s.at[stage, d], tr_r.at[stage, src], partner).wait_recv()
        for copy in trace_axis_copies(stage, axis):
            copy.wait_send()
        vsend[stage + 1] = (vaxis[stage, 0] + vaxis[stage, 1]) + (vaxis[stage, 2] + vaxis[stage, 3])

    def fin_copy(j, core):
        ref = fin.at[core, pl.ds(j * CH, CH)]
        return rcopy(ref, ref, fx_s.at[j], fx_r.at[j], partner)

    def make_step(s):
        step = {}
        an, bn, cn = ROLES[s]
        a, b, c = pos[an], pos[bn], pos[cn]
        d = wrap(b - c)
        root = d == 0
        up, down, far = wrap(a + 1), wrap(a - 1), wrap(a + 2)

        def rows(j):
            return pl.ds(j * CH, CH)

        def half_rows(j, direction):
            return pl.ds(j * CH + direction * HALF, HALF)

        def sign(direction):
            return 1 - 2 * direction

        def ag_copy(direction, j):
            ref = pbuf.at[s, c, k, rows(j)]
            return rcopy(ref, ref, ag_s.at[s, direction, j], ag_r.at[s, direction, j], at(cn, sign(direction)))

        def ag_wait(direction, j):
            ref = pbuf.at[s, wrap(c - sign(direction)), k, rows(j)]
            rcopy(ref, ref, ag_s.at[s, direction, j], ag_r.at[s, direction, j], partner).wait_recv()

        def af_copy(direction, j):
            ref = pbuf.at[s, wrap(c - sign(direction)), k, half_rows(j, direction)]
            return rcopy(ref, ref, af_s.at[s, direction, j], af_r.at[s, direction, j], at(cn, sign(direction)))

        def af_wait(direction, j):
            ref = pbuf.at[s, wrap(c + 2), k, half_rows(j, direction)]
            rcopy(ref, ref, af_s.at[s, direction, j], af_r.at[s, direction, j], partner).wait_recv()

        def cx_copy(j, i):
            ref = pbuf.at[s, wrap(c + OFFSETS[i]), k, rows(j)]
            return rcopy(ref, ref, cx_s.at[s, j, i], cx_r.at[s, j, i], partner)

        def cx_wait(j, i):
            ref = pbuf.at[s, wrap(c + OFFSETS[i]), other, rows(j)]
            rcopy(ref, ref, cx_s.at[s, j, i], cx_r.at[s, j, i], partner).wait_recv()

        def bc_copy(direction, seq, from_root):
            j = lax.div(seq, 4)
            part = lax.rem(seq, 4)
            q = wrap(c + jnp.where(part == 1, -1, jnp.where(part == 2, 1, jnp.where(part == 3, 2, 0))))
            place = pl.ds(pl.multiple_of(j * CH + direction * HALF, HALF), HALF)
            dst = qbuf.at[s, q, place]
            src = pbuf.at[s, q, k, place] if from_root else dst
            return rcopy(src, dst, bc_s.at[s, direction, seq], bc_r.at[s, direction, seq], at(bn, sign(direction)))

        def bc_root(*seqs):
            @pl.when(root)
            def _():
                for seq in seqs:
                    bc_copy(0, jnp.int32(seq), True).start()
                    bc_copy(1, jnp.int32(seq), True).start()

        def bc_tick(tick):
            for direction in (0, 1):
                hops = d - 1 if direction == 0 else 3 - d
                seq = tick - LAG * hops

                @pl.when(jnp.logical_and(d > 0, jnp.logical_and(seq >= 0, seq < 16)))
                def _():
                    copy = bc_copy(direction, seq, False)
                    copy.wait_recv()

                    @pl.when(hops < 2)
                    def _():
                        copy.start()

        def ready(j):
            ag_copy(0, j).start()
            ag_copy(1, j).start()
            bc_root(4 * j)
            cx_copy(j, 0).start()

        def direct(j):
            for direction in (0, 1):
                ag_wait(direction, j)
                af_copy(direction, j).start()
            if s == 0 and j < 2:
                ready(j + 2)
            cx_copy(j, 1).start()
            cx_copy(j, 2).start()
            bc_root(4 * j + 1, 4 * j + 2)

        def handed(j):
            for direction in (0, 1):
                af_wait(direction, j)
            cx_copy(j, 3).start()
            bc_root(4 * j + 3)

        def split_p(j):
            for i in range(4):
                cx_wait(j, i)

            @pl.loop(0, 8)
            def _(i):
                row = pl.multiple_of(j * 8 * CH + i * CH, CH)
                high, low = split(pbuf[s, lax.div(i, 2), lax.rem(i, 2), rows(j)])
                phi[s % 2, pl.ds(row, CH), :] = high
                plo[s % 2, pl.ds(row, CH), :] = low

        def split_q(j):
            def halves(read):
                for q in range(4):
                    high, low = split(read(q))
                    qcat[j, q * CH:(q + 1) * CH, :] = high
                    qcat[j, SLAB + q * CH:SLAB + (q + 1) * CH, :] = low

            @pl.when(root)
            def _():
                halves(lambda q: pbuf[s, q, k, rows(j)])

            @pl.when(jnp.logical_not(root))
            def _():
                halves(lambda q: qbuf[s, q, rows(j)])

        def product(j, first, last):
            weight = br[s].astype(F32)
            scale = 1.0 - 2.0 * weight
            linear = 2.0 * weight * (a == b).astype(F32)

            @pl.loop(first, last)
            def _(n):
                lanes = pl.ds(pl.multiple_of(n * 256, 256), 256)
                both = nt_dot(qcat[j], phi[s % 2, lanes, :])
                value = both[:SLAB] + both[SLAB:] + nt_dot(qcat[j, :SLAB, :], plo[s % 2, lanes, :])
                same = qcat[j, :SLAB, lanes].astype(F32) + qcat[j, SLAB:, lanes].astype(F32)
                obuf[s, j, :, lanes] = scale * value + linear * same

        def send_out(j):
            for i in (0, 1):
                for direction in (0, 1):
                    rs_copy(direction, i, j).start()

        def out_half(q, second):
            return pl.ds(pl.multiple_of(q * CH + second * HALF, HALF), HALF)

        def rs_copy(direction, i, j):
            near = up if direction == 0 else down
            if i == 0:
                src, dst = obuf.at[s, j, out_half(far, direction)], r1.at[s, direction, j]
            else:
                second = 1 - direction if i == 1 else direction
                src = obuf.at[s, j, out_half(near, second)]
                dst = r2.at[s, direction, j, pl.ds(second * HALF, HALF)]
            return rcopy(src, dst, rs_s.at[s, direction, j, i], rs_r.at[s, direction, j, i], at(an, sign(direction)))

        def add_on(j):
            for direction in (0, 1):
                rs_copy(direction, 0, j).wait_recv()
                place = out_half(up if direction == 0 else down, direction)
                obuf[s, j, place, :] = obuf[s, j, place, :] + r1[s, direction, j]
                rs_copy(direction, 2, j).start()

        def mask():
            pattern_wait(s)
            line = lax.broadcasted_iota(jnp.int32, (SLAB, 16), 0)
            block = lax.broadcasted_iota(jnp.int32, (SLAB, 16), 1)
            pick = (block == a * 4 + k * 2 + line // BS).astype(F32)
            left = lax.broadcasted_iota(jnp.int32, (128, 256), 0)
            right = lax.broadcasted_iota(jnp.int32, (128, 256), 1)
            chosen = [jnp.dot(pick, gbuf[s, q], preferred_element_type=F32) for q in range(4)]
            for pair in range(2):
                value = jnp.zeros((SLAB, 256), F32)
                for q in range(4):
                    wanted = (right % 64) // CH * 2 + pair
                    spread = jnp.logical_and(right // 64 == q, left == wanted).astype(F32)
                    value = value + jnp.dot(chosen[q], spread, preferred_element_type=F32)
                for i in (2 * pair, 2 * pair + 1):
                    mbuf[s, :, i * 256:(i + 1) * 256] = value

        def finish(j):
            for i in (1, 2):
                for direction in (0, 1):
                    rs_copy(direction, i, j).wait_recv()
            place = pl.ds(pl.multiple_of(a * CH, CH), CH)
            value = obuf[s, j, place, :] + (r2[s, 0, j] + r2[s, 1, j])
            if s < 2:
                pbuf[s + 1, a, k, rows(j), :] = value * mbuf[s, rows(j), :]
            else:
                fin[k, rows(j), :] = value
                fin_copy(j, k).start()

        def sent():
            for direction in (0, 1):
                for j in range(4):
                    ag_copy(direction, j).wait_send()
                    af_copy(direction, j).wait_send()

                @pl.when(d != (3 if direction == 0 else 1))
                def _():
                    for seq in range(16):
                        bc_copy(direction, jnp.int32(seq), False).wait_send()
            for j in range(4):
                for i in range(4):
                    cx_copy(j, i).wait_send()
            if s == 0:
                for copy in pattern_copies():
                    copy.wait_send()

        def rs_sent():
            for direction in (0, 1):
                for j in range(4):
                    for i in range(3):
                        rs_copy(direction, i, j).wait_send()

        step.update(locals())
        return step

    steps = [make_step(s) for s in range(STEPS)]
    steps[0]["ready"](0)
    steps[0]["ready"](1)
    for copy in pattern_copies():
        copy.start()

    events = {}

    def due(name, time, act, needs=()):
        time = max([time] + [events[need][0] for need in needs])
        events[name] = (time, len(events), act)

    def end_unit(s, j):
        steps[s]["finish"](j)
        if s + 1 < STEPS:
            steps[s + 1]["ready"](j)

    call = functools.partial
    for s in range(STEPS):
        now = steps[s]
        zero = START_AT[s]
        plan = ARRIVE[min(s, 1)]
        for j in range(4):
            begun = [("end", s - 1, j)] if s else []
            due(("direct", s, j), zero + plan["direct"][j], call(now["direct"], j), begun)
            due(("handed", s, j), zero + plan["handed"][j], call(now["handed"], j), [("direct", s, j)])
            due(("split_p", s, j), zero + plan["split_p"][j], call(now["split_p"], j), [("handed", s, j)])
        tick = plan["tick"]
        for t in range(16 + 2 * LAG):
            due(("tick", s, t), zero + tick(t), call(now["bc_tick"], t), [("tick", s, t - 1)] if t else begun)
        if s < 2:
            due(("mask", s), zero + 13.0, now["mask"], [("end", s - 1, 3)] if s else [])
        for j in range(4):
            due(("split_q", s, j), zero + plan["piece"][j], call(now["split_q"], j),
                [("tick", s, 4 * j + 3 + 2 * LAG), ("handed", s, j)])
            early = 3 if j == 0 else 0
            if early:
                due(("early", s, j), zero + plan["piece"][j], call(now["product"], j, 0, early),
                    [("split_q", s, j), ("split_p", s, early - 1)])
            due(("product", s, j), zero + plan["product"][j], call(now["product"], j, early, 4),
                [("split_q", s, j), ("split_p", s, 3)] + ([("early", s, j)] if early else []))
            due(("send_out", s, j), zero + plan["product"][j], call(now["send_out"], j), [("product", s, j)])
            due(("add_on", s, j), zero + plan["add_on"][j], call(now["add_on"], j), [("send_out", s, j)])
            due(("end", s, j), zero + plan["finish"][j], call(end_unit, s, j),
                [("add_on", s, j)] + ([("mask", s)] if s < 2 else []))
        due(("sum", s), zero + plan["sum"], call(square_sum, s, now["c"]), [("end", s - 1, 3)] if s else [])
        if s > 0:
            due(("sent", s - 1), zero + 16.0, steps[s - 1]["sent"], [("end", s - 1, 3)])
            due(("rs_sent", s - 1), zero + 20.0, steps[s - 1]["rs_sent"], [("end", s - 1, 3)])
        if s == 2:
            chain = [
                (0.0, lambda: trace_core().start()),
                (17.0, trace_core_end), (17.0, call(trace_axis_start, 1, "x")),
                (22.0, call(trace_axis_end, 1, "x")), (22.0, call(trace_axis_start, 2, "y")),
                (29.0, call(trace_axis_end, 2, "y")), (29.0, call(trace_axis_start, 3, "z")),
                (38.0, call(trace_axis_end, 3, "z")),
            ]
            before = ("sum", 2)
            for n, (time, act) in enumerate(chain):
                due(("trace", n), zero + time, act, [before])
                before = ("trace", n)
            due(("sent", s), zero + 39.0, now["sent"], [("tick", s, 15 + 2 * LAG), ("handed", s, 3)])
    for _, _, act in sorted(events.values(), key=lambda event: event[:2]):
        act()
    tr_out[...] = vsend[4]
    left = lax.broadcasted_iota(jnp.int32, (128, 256), 0)
    right = lax.broadcasted_iota(jnp.int32, (128, 256), 1)
    spread = (left == right // BS).astype(F32)
    line = lax.broadcasted_iota(jnp.int32, (128, 16), 0)
    block = lax.broadcasted_iota(jnp.int32, (128, 16), 1)
    steps[2]["rs_sent"]()
    for j in range(4):
        fin_copy(j, other).wait_recv()
    for i in range(8):
        here = [line // CH == n for n in range(4)]
        wanted = sum(jnp.where(here[n], row // BS, 0) for n, row in enumerate(lane_rows(i)))
        pick = (block == wanted).astype(F32)
        chosen = jnp.dot(pick, patf[...], preferred_element_type=F32)
        mask = jnp.dot(chosen, spread, preferred_element_type=F32)
        for half in range(2):
            lanes = slice(half * 128, (half + 1) * 128)
            part = fin[half, :, i * 128:(i + 1) * 128].T * mask[:, lanes]
            for n, row in enumerate(lane_rows(i)):
                out[row:row + CH, lanes] = part[n * CH:(n + 1) * CH]
    for j in range(4):
        fin_copy(j, k).wait_send()


def per_device(density, pattern, branches):
    vmem = pl.BlockSpec(memory_space=pltpu.VMEM)
    dma = pltpu.SemaphoreType.DMA
    purified, traces = pl.pallas_call(
        body,
        out_shape=(
            jax.ShapeDtypeStruct((BLK, 256), F32),
            jax.ShapeDtypeStruct((8, 128), F32),
        ),
        in_specs=[vmem, vmem, pl.BlockSpec(memory_space=pltpu.SMEM)],
        out_specs=(vmem, vmem),
        scratch_shapes=[
            pltpu.VMEM((STEPS, 4, 2, SLAB, BLK), F32),
            pltpu.VMEM((STEPS, 4, SLAB, BLK), F32),
            pltpu.VMEM((2, BLK, BLK), BF16),
            pltpu.VMEM((2, BLK, BLK), BF16),
            pltpu.VMEM((4, 2 * SLAB, BLK), BF16),
            pltpu.VMEM((STEPS, 4, SLAB, BLK), F32),
            pltpu.VMEM((STEPS, 2, 4, HALF, BLK), F32),
            pltpu.VMEM((STEPS, 2, 4, CH, BLK), F32),
            pltpu.VMEM((16, 128), F32),
            pltpu.VMEM((2, 4, 16, 128), F32),
            pltpu.VMEM((2, SLAB, BLK), F32),
            pltpu.VMEM((5, 8, 128), F32),
            pltpu.VMEM((8, 128), F32),
            pltpu.VMEM((4, 4, 8, 128), F32),
            pltpu.VMEM((2, SLAB, BLK), F32),
            dma((STEPS, 2, 4)), dma((STEPS, 2, 4)),
            dma((STEPS, 2, 4)), dma((STEPS, 2, 4)),
            dma((STEPS, 4, 4)), dma((STEPS, 4, 4)),
            dma((STEPS, 2, 16)), dma((STEPS, 2, 16)),
            dma((STEPS, 2, 4, 3)), dma((STEPS, 2, 4, 3)),
            dma((2, 4)), dma((2, 4)),
            dma((4, 4)), dma((4, 4)),
            dma((4,)), dma((4,)),
        ],
        compiler_params=pltpu.CompilerParams(
            collective_id=0, has_side_effects=True, vmem_limit_bytes=56 * 2**20
        ),
        name="purify",
    )(density, pattern, branches)
    return purified, traces[:STEPS, 0]


def solution(mesh):
    return jax.shard_map(
        per_device,
        mesh=mesh,
        in_specs=(P("row", "col"), P("row", "col"), P()),
        out_specs=(P("row", "col"), P()),
        check_vma=False,
    )
```

```python
import functools

import jax
import jax.numpy as jnp
from jax import lax
from jax.experimental import pallas as pl
from jax.experimental.pallas import tpu as pltpu
from jax.sharding import PartitionSpec as P

MESH = pl.DeviceIdType.MESH
STEPS = 3
BS = 64
BLK = 1024
SLAB = 128
CH = 32
HALF = 16
OFFSETS = (0, -1, 1, 2)
ORDER = {
    "direct": (
        (3, 5, 15, 25),
        (92, 101, 111, 119),
        (182, 189, 199, 207),
    ),
    "handed": (
        (8, 18, 30, 34),
        (97, 108, 118, 130),
        (188, 197, 212, 224),
    ),
    "split_p": (
        (14, 21, 35, 39),
        (98, 113, 127, 138),
        (191, 202, 218, 229),
    ),
    "split_q": (
        (46, 60, 73, 81),
        (123, 144, 162, 174),
        (215, 237, 254, 265),
    ),
    "product": (
        (48, 50, 51, 53, 61, 62, 63, 66, 74, 75, 76, 77, 82, 83, 84, 86),
        (124, 128, 129, 139, 145, 146, 147, 148, 163, 164, 165, 166, 175, 176, 177, 178),
        (216, 217, 221, 231, 238, 239, 240, 243, 255, 257, 259, 260, 266, 267, 268, 269),
    ),
    "send_out": (
        (54, 67, 78, 87),
        (140, 150, 167, 180),
        (232, 245, 261, 271),
    ),
    "add_on": (
        (64, 79, 90, 91),
        (156, 161, 179, 183),
        (249, 252, 272, 273),
    ),
    "end": (
        (71, 89, 94, 96),
        (171, 172, 185, 193),
        (263, 270, 274, 275),
    ),
    "bc": (
        (0, 1, 13, 4, 11, 22, 6, 17, 26, 24, 38, 45, 2, 7, 9, 12, 23, 32, 16, 28, 37, 36, 49, 58, 10, 19, 29, 27, 40, 52, 31, 43, 56, 47, 65, 72, 20, 33, 42, 41, 57, 68, 44, 59, 70, 55, 69, 80),
        (85, 88, 100, 95, 104, 114, 99, 106, 116, 102, 112, 120, 93, 103, 109, 105, 115, 131, 107, 121, 134, 117, 133, 143, 110, 125, 136, 126, 141, 153, 132, 149, 158, 135, 152, 159, 122, 137, 155, 142, 157, 169, 151, 160, 170, 154, 168, 173),
        (181, 184, 192, 187, 196, 206, 190, 201, 210, 194, 205, 214, 186, 195, 204, 198, 209, 222, 200, 213, 226, 208, 225, 236, 203, 220, 234, 219, 233, 247, 223, 242, 251, 228, 246, 253, 211, 227, 241, 230, 248, 258, 235, 250, 262, 244, 256, 264),
    ),
}
ROLES = (("x", "z", "y"), ("z", "y", "x"), ("y", "x", "z"))
F32 = jnp.float32
BF16 = jnp.bfloat16


def nt_dot(left, right):
    return lax.dot_general(left, right, (((1,), (1,)), ((), ())), preferred_element_type=F32)


def split(value):
    high = value.astype(BF16)
    return high, (value - high.astype(F32)).astype(BF16)


def lane_rows(i):
    unit = i // 2
    return [(2 * (i % 2) + q) * 256 + core * SLAB + unit * CH for q in (0, 1) for core in (0, 1)]


def body(
    dens, pat, br, out, tr_out,
    pbuf, qbuf, phi, plo, qcat, obuf, r1, r2, patf, gbuf, mbuf, vsend, vcore, vaxis, fin,
    ag_s, ag_r, af_s, af_r, cx_s, cx_r, bc_s, bc_r, rs_s, rs_r, pt_s, pt_r, tr_s, tr_r, fx_s, fx_r,
):
    col = lax.axis_index("col")
    k = lax.axis_index("depth")
    pos = {"x": lax.axis_index("row"), "y": lax.rem(col, 4), "z": lax.div(col, 4)}
    other = 1 - k

    def wrap(value):
        return lax.rem(value + 8, 4)

    def device(x, y, z, core):
        return (x, z * 4 + y, core)

    def at(axis, delta):
        place = dict(pos)
        place[axis] = wrap(place[axis] + delta)
        return device(place["x"], place["y"], place["z"], k)

    partner = device(pos["x"], pos["y"], pos["z"], other)

    def rcopy(src, dst, send, recv, dev):
        return pltpu.make_async_remote_copy(
            src_ref=src, dst_ref=dst, send_sem=send, recv_sem=recv, device_id=dev, device_id_type=MESH
        )

    barrier = pltpu.get_barrier_semaphore()
    greet = [partner]
    for axis in ("x", "y", "z"):
        for delta in (1, -1, 2):
            greet.append(at(axis, delta))
    for i in range(4):
        greet.append(device(pos["y"], i, pos["z"], other))
        greet.append(device(pos["x"], i, pos["y"], other))
    for dev in greet:
        pl.semaphore_signal(barrier, inc=1, device_id=dev, device_id_type=MESH)

    for i in range(8):
        mine = pl.ds(pl.multiple_of(k * 128, 128), 128)
        piece = jnp.concatenate([dens[row:row + CH, mine] for row in lane_rows(i)], axis=0)
        pbuf[0, pos["y"], k, :, i * 128:(i + 1) * 128] = piece.T
    patf[...] = jnp.zeros_like(patf)
    vsend[0] = jnp.zeros((8, 128), F32)
    patf[:, 0:4] = pat[...].astype(F32)
    pl.semaphore_wait(barrier, len(greet))

    def pattern_copies():
        found = []
        for i in range(4):
            found.append(rcopy(patf, gbuf.at[0, pos["y"]], pt_s.at[0, i], pt_r.at[0, pos["y"]],
                               device(i, pos["x"], pos["z"], other)))
            found.append(rcopy(patf, gbuf.at[1, pos["y"]], pt_s.at[1, i], pt_r.at[1, pos["y"]],
                               device(pos["x"], pos["z"], i, other)))
        return found

    def pattern_wait(s):
        for i in range(4):
            rcopy(patf, gbuf.at[s, i], pt_s.at[s, i], pt_r.at[s, i], partner).wait_recv()

    def square_sum(s, slab):
        total = jnp.zeros((1, BLK), F32)
        for i in range(4):
            part = pbuf[s, slab, k, i * CH:(i + 1) * CH, :]
            total = total + jnp.sum(part * part, axis=0, keepdims=True)
        vsend[0, s:s + 1, :] = jnp.broadcast_to(jnp.sum(total, axis=1, keepdims=True), (1, 128))

    def trace_core():
        return rcopy(vsend.at[0], vcore, tr_s.at[0, 0], tr_r.at[0, 0], partner)

    def trace_core_end():
        trace_core().wait()
        vsend[1] = vsend[0] + vcore[...]

    def trace_axis_copies(stage, axis):
        me = pos[axis]
        return [
            rcopy(vsend.at[stage], vaxis.at[stage, me], tr_s.at[stage, d], tr_r.at[stage, me], at(axis, d))
            for d in (1, 2, 3)
        ]

    def trace_axis_start(stage, axis):
        for copy in trace_axis_copies(stage, axis):
            copy.start()
        vaxis[stage, pos[axis]] = vsend[stage]

    def trace_axis_end(stage, axis):
        for d in (1, 2, 3):
            src = wrap(pos[axis] + d)
            rcopy(vsend.at[stage], vaxis.at[stage, src], tr_s.at[stage, d], tr_r.at[stage, src], partner).wait_recv()
        for copy in trace_axis_copies(stage, axis):
            copy.wait_send()
        vsend[stage + 1] = (vaxis[stage, 0] + vaxis[stage, 1]) + (vaxis[stage, 2] + vaxis[stage, 3])

    def fin_copy(j, core):
        ref = fin.at[core, pl.ds(j * CH, CH)]
        return rcopy(ref, ref, fx_s.at[j], fx_r.at[j], partner)

    def make_step(s):
        step = {}
        an, bn, cn = ROLES[s]
        a, b, c = pos[an], pos[bn], pos[cn]
        d = wrap(b - c)
        root = d == 0
        up, down, far = wrap(a + 1), wrap(a - 1), wrap(a + 2)

        def rows(j):
            return pl.ds(j * CH, CH)

        def half_rows(j, direction):
            return pl.ds(j * CH + direction * HALF, HALF)

        def sign(direction):
            return 1 - 2 * direction

        def ag_copy(direction, j):
            ref = pbuf.at[s, c, k, rows(j)]
            return rcopy(ref, ref, ag_s.at[s, direction, j], ag_r.at[s, direction, j], at(cn, sign(direction)))

        def ag_wait(direction, j):
            ref = pbuf.at[s, wrap(c - sign(direction)), k, rows(j)]
            rcopy(ref, ref, ag_s.at[s, direction, j], ag_r.at[s, direction, j], partner).wait_recv()

        def af_copy(direction, j):
            ref = pbuf.at[s, wrap(c - sign(direction)), k, half_rows(j, direction)]
            return rcopy(ref, ref, af_s.at[s, direction, j], af_r.at[s, direction, j], at(cn, sign(direction)))

        def af_wait(direction, j):
            ref = pbuf.at[s, wrap(c + 2), k, half_rows(j, direction)]
            rcopy(ref, ref, af_s.at[s, direction, j], af_r.at[s, direction, j], partner).wait_recv()

        def cx_copy(j, i):
            ref = pbuf.at[s, wrap(c + OFFSETS[i]), k, rows(j)]
            return rcopy(ref, ref, cx_s.at[s, j, i], cx_r.at[s, j, i], partner)

        def cx_wait(j, i):
            ref = pbuf.at[s, wrap(c + OFFSETS[i]), other, rows(j)]
            rcopy(ref, ref, cx_s.at[s, j, i], cx_r.at[s, j, i], partner).wait_recv()

        def bc_copy(direction, j, i, from_root):
            q = wrap(c + OFFSETS[i])
            place = half_rows(j, direction)
            dst = qbuf.at[s, q, place]
            src = pbuf.at[s, q, k, place] if from_root else dst
            return rcopy(src, dst, bc_s.at[s, direction, j, i], bc_r.at[s, direction, j, i], at(bn, sign(direction)))

        def bc_root(j, *parts):
            @pl.when(root)
            def _():
                for i in parts:
                    bc_copy(0, j, i, True).start()
                    bc_copy(1, j, i, True).start()

        def bc_hop(hop, j, i):
            def hand_on(*directions):
                for direction in directions:
                    copy = bc_copy(direction, j, i, False)
                    copy.wait_recv()
                    if hop < 3:
                        copy.start()

            if hop == 2:
                pl.when(d == 2)(functools.partial(hand_on, 0, 1))
            else:
                pl.when(d == hop)(functools.partial(hand_on, 0))
                pl.when(d == 4 - hop)(functools.partial(hand_on, 1))

        def ready(j):
            ag_copy(0, j).start()
            ag_copy(1, j).start()
            bc_root(j, 0)
            cx_copy(j, 0).start()

        def direct(j):
            for direction in (0, 1):
                ag_wait(direction, j)
                af_copy(direction, j).start()
            if s == 0 and j < 2:
                ready(j + 2)
            cx_copy(j, 1).start()
            cx_copy(j, 2).start()
            bc_root(j, 1, 2)

        def handed(j):
            for direction in (0, 1):
                af_wait(direction, j)
            cx_copy(j, 3).start()
            bc_root(j, 3)

        def split_p(j):
            for i in range(4):
                cx_wait(j, i)

            @pl.loop(0, 8)
            def _(i):
                row = pl.multiple_of(j * 8 * CH + i * CH, CH)
                high, low = split(pbuf[s, lax.div(i, 2), lax.rem(i, 2), rows(j)])
                phi[s % 2, pl.ds(row, CH), :] = high
                plo[s % 2, pl.ds(row, CH), :] = low

        def split_q(j):
            def halves(read):
                for q in range(4):
                    high, low = split(read(q))
                    qcat[j, q * CH:(q + 1) * CH, :] = high
                    qcat[j, SLAB + q * CH:SLAB + (q + 1) * CH, :] = low

            @pl.when(root)
            def _():
                halves(lambda q: pbuf[s, q, k, rows(j)])

            @pl.when(jnp.logical_not(root))
            def _():
                halves(lambda q: qbuf[s, q, rows(j)])

        def product(j, first, last):
            weight = br[s].astype(F32)
            scale = 1.0 - 2.0 * weight
            linear = 2.0 * weight * (a == b).astype(F32)

            @pl.loop(first, last)
            def _(n):
                lanes = pl.ds(pl.multiple_of(n * 256, 256), 256)
                both = nt_dot(qcat[j], phi[s % 2, lanes, :])
                value = both[:SLAB] + both[SLAB:] + nt_dot(qcat[j, :SLAB, :], plo[s % 2, lanes, :])
                same = qcat[j, :SLAB, lanes].astype(F32) + qcat[j, SLAB:, lanes].astype(F32)
                obuf[s, j, :, lanes] = scale * value + linear * same

        def send_out(j):
            for i in (0, 1):
                for direction in (0, 1):
                    rs_copy(direction, i, j).start()

        def out_half(q, second):
            return pl.ds(pl.multiple_of(q * CH + second * HALF, HALF), HALF)

        def rs_copy(direction, i, j):
            near = up if direction == 0 else down
            if i == 0:
                src, dst = obuf.at[s, j, out_half(far, direction)], r1.at[s, direction, j]
            else:
                second = 1 - direction if i == 1 else direction
                src = obuf.at[s, j, out_half(near, second)]
                dst = r2.at[s, direction, j, pl.ds(second * HALF, HALF)]
            return rcopy(src, dst, rs_s.at[s, direction, j, i], rs_r.at[s, direction, j, i], at(an, sign(direction)))

        def add_on(j):
            for direction in (0, 1):
                rs_copy(direction, 0, j).wait_recv()
                place = out_half(up if direction == 0 else down, direction)
                obuf[s, j, place, :] = obuf[s, j, place, :] + r1[s, direction, j]
                rs_copy(direction, 2, j).start()

        def mask():
            pattern_wait(s)
            line = lax.broadcasted_iota(jnp.int32, (SLAB, 16), 0)
            block = lax.broadcasted_iota(jnp.int32, (SLAB, 16), 1)
            pick = (block == a * 4 + k * 2 + line // BS).astype(F32)
            left = lax.broadcasted_iota(jnp.int32, (128, 256), 0)
            right = lax.broadcasted_iota(jnp.int32, (128, 256), 1)
            chosen = [jnp.dot(pick, gbuf[s, q], preferred_element_type=F32) for q in range(4)]
            for pair in range(2):
                value = jnp.zeros((SLAB, 256), F32)
                for q in range(4):
                    wanted = (right % 64) // CH * 2 + pair
                    spread = jnp.logical_and(right // 64 == q, left == wanted).astype(F32)
                    value = value + jnp.dot(chosen[q], spread, preferred_element_type=F32)
                for i in (2 * pair, 2 * pair + 1):
                    mbuf[s, :, i * 256:(i + 1) * 256] = value

        def finish(j):
            for i in (1, 2):
                for direction in (0, 1):
                    rs_copy(direction, i, j).wait_recv()
            place = pl.ds(pl.multiple_of(a * CH, CH), CH)
            value = obuf[s, j, place, :] + (r2[s, 0, j] + r2[s, 1, j])
            if s < 2:
                pbuf[s + 1, a, k, rows(j), :] = value * mbuf[s, rows(j), :]
            else:
                fin[k, rows(j), :] = value
                fin_copy(j, k).start()

        def sent():
            for direction in (0, 1):
                for j in range(4):
                    ag_copy(direction, j).wait_send()
                    af_copy(direction, j).wait_send()

                @pl.when(d != (3 if direction == 0 else 1))
                def _():
                    for j in range(4):
                        for i in range(4):
                            bc_copy(direction, j, i, False).wait_send()
            for j in range(4):
                for i in range(4):
                    cx_copy(j, i).wait_send()
            if s == 0:
                for copy in pattern_copies():
                    copy.wait_send()

        def rs_sent():
            for direction in (0, 1):
                for j in range(4):
                    for i in range(3):
                        rs_copy(direction, i, j).wait_send()

        step.update(locals())
        return step

    steps = [make_step(s) for s in range(STEPS)]
    steps[0]["ready"](0)
    steps[0]["ready"](1)
    for copy in pattern_copies():
        copy.start()

    events = {}

    def due(name, time, act, needs=()):
        time = max([time] + [events[need][0] for need in needs])
        events[name] = (time, len(events), act)

    def end_unit(s, j):
        steps[s]["finish"](j)
        if s + 1 < STEPS:
            steps[s + 1]["ready"](j)

    call = functools.partial
    units = range(4)
    hops = (1, 2, 3)
    for s in range(STEPS):
        now = steps[s]

        def place(kind, n):
            return ORDER[kind][s][n]

        for j in units:
            begun = [("end", s - 1, j)] if s else []
            due(("direct", s, j), place("direct", j), call(now["direct"], j), begun)
            due(("handed", s, j), place("handed", j), call(now["handed"], j), [("direct", s, j)])
            due(("split_p", s, j), place("split_p", j), call(now["split_p"], j), [("handed", s, j)])
            for i in units:
                first = begun if i == 0 else [("handed" if i == 3 else "direct", s, j)]
                for hop in hops:
                    needs = [("bc", s, j, i, hop - 1)] if hop > 1 else first
                    due(("bc", s, j, i, hop), place("bc", j * 12 + i * 3 + hop - 1), call(now["bc_hop"], hop, j, i), needs)
        if s < 2:
            due(("mask", s), place("direct", 3), now["mask"], [("direct", s, 3)])
        for j in units:
            due(("split_q", s, j), place("split_q", j), call(now["split_q"], j),
                [("bc", s, j, i, hop) for i in units for hop in hops] + [("handed", s, j)])
            before = ("split_q", s, j)
            for n in units:
                due(("product", s, j, n), place("product", j * 4 + n), call(now["product"], j, n, n + 1),
                    [before, ("split_p", s, n)])
                before = ("product", s, j, n)
            due(("send_out", s, j), place("send_out", j), call(now["send_out"], j), [before])
            due(("add_on", s, j), place("add_on", j), call(now["add_on"], j), [("send_out", s, j)])
            due(("end", s, j), place("end", j), call(end_unit, s, j),
                [("add_on", s, j)] + ([("mask", s)] if s < 2 else []))
        late = [("end", s - 1, n) for n in units] if s else []
        due(("sum", s), place("direct", 2), call(square_sum, s, now["c"]), late)
        if s > 0:
            due(("sent", s - 1), place("handed", 2), steps[s - 1]["sent"], late + [("direct", s, 3)])
            due(("rs_sent", s - 1), place("handed", 3), steps[s - 1]["rs_sent"], late + [("direct", s, 3)])
        if s == 2:
            chain = [
                (place("direct", 2), lambda: trace_core().start()),
                (place("handed", 2), trace_core_end), (place("handed", 2), call(trace_axis_start, 1, "x")),
                (place("split_p", 3), call(trace_axis_end, 1, "x")), (place("split_p", 3), call(trace_axis_start, 2, "y")),
                (place("send_out", 2), call(trace_axis_end, 2, "y")), (place("send_out", 2), call(trace_axis_start, 3, "z")),
                (place("add_on", 3), call(trace_axis_end, 3, "z")),
            ]
            before = ("sum", 2)
            for n, (time, act) in enumerate(chain):
                due(("trace", n), time, act, [before])
                before = ("trace", n)
            due(("sent", s), place("add_on", 3), now["sent"], [("split_q", s, j) for j in units])
    for _, _, act in sorted(events.values(), key=lambda event: event[:2]):
        act()
    tr_out[...] = vsend[4]
    left = lax.broadcasted_iota(jnp.int32, (128, 256), 0)
    right = lax.broadcasted_iota(jnp.int32, (128, 256), 1)
    spread = (left == right // BS).astype(F32)
    line = lax.broadcasted_iota(jnp.int32, (128, 16), 0)
    block = lax.broadcasted_iota(jnp.int32, (128, 16), 1)
    steps[2]["rs_sent"]()
    for j in range(4):
        fin_copy(j, other).wait_recv()
    for i in range(8):
        here = [line // CH == n for n in range(4)]
        wanted = sum(jnp.where(here[n], row // BS, 0) for n, row in enumerate(lane_rows(i)))
        pick = (block == wanted).astype(F32)
        chosen = jnp.dot(pick, patf[...], preferred_element_type=F32)
        mask = jnp.dot(chosen, spread, preferred_element_type=F32)
        for half in range(2):
            lanes = slice(half * 128, (half + 1) * 128)
            part = fin[half, :, i * 128:(i + 1) * 128].T * mask[:, lanes]
            for n, row in enumerate(lane_rows(i)):
                out[row:row + CH, lanes] = part[n * CH:(n + 1) * CH]
    for j in range(4):
        fin_copy(j, k).wait_send()


def per_device(density, pattern, branches):
    vmem = pl.BlockSpec(memory_space=pltpu.VMEM)
    dma = pltpu.SemaphoreType.DMA
    purified, traces = pl.pallas_call(
        body,
        out_shape=(
            jax.ShapeDtypeStruct((BLK, 256), F32),
            jax.ShapeDtypeStruct((8, 128), F32),
        ),
        in_specs=[vmem, vmem, pl.BlockSpec(memory_space=pltpu.SMEM)],
        out_specs=(vmem, vmem),
        scratch_shapes=[
            pltpu.VMEM((STEPS, 4, 2, SLAB, BLK), F32),
            pltpu.VMEM((STEPS, 4, SLAB, BLK), F32),
            pltpu.VMEM((2, BLK, BLK), BF16),
            pltpu.VMEM((2, BLK, BLK), BF16),
            pltpu.VMEM((4, 2 * SLAB, BLK), BF16),
            pltpu.VMEM((STEPS, 4, SLAB, BLK), F32),
            pltpu.VMEM((STEPS, 2, 4, HALF, BLK), F32),
            pltpu.VMEM((STEPS, 2, 4, CH, BLK), F32),
            pltpu.VMEM((16, 128), F32),
            pltpu.VMEM((2, 4, 16, 128), F32),
            pltpu.VMEM((2, SLAB, BLK), F32),
            pltpu.VMEM((5, 8, 128), F32),
            pltpu.VMEM((8, 128), F32),
            pltpu.VMEM((4, 4, 8, 128), F32),
            pltpu.VMEM((2, SLAB, BLK), F32),
            dma((STEPS, 2, 4)), dma((STEPS, 2, 4)),
            dma((STEPS, 2, 4)), dma((STEPS, 2, 4)),
            dma((STEPS, 4, 4)), dma((STEPS, 4, 4)),
            dma((STEPS, 2, 4, 4)), dma((STEPS, 2, 4, 4)),
            dma((STEPS, 2, 4, 3)), dma((STEPS, 2, 4, 3)),
            dma((2, 4)), dma((2, 4)),
            dma((4, 4)), dma((4, 4)),
            dma((4,)), dma((4,)),
        ],
        compiler_params=pltpu.CompilerParams(
            collective_id=0, has_side_effects=True, vmem_limit_bytes=56 * 2**20
        ),
        name="purify",
    )(density, pattern, branches)
    return purified, traces[:STEPS, 0]


def solution(mesh):
    return jax.shard_map(
        per_device,
        mesh=mesh,
        in_specs=(P("row", "col"), P("row", "col"), P()),
        out_specs=(P("row", "col"), P()),
        check_vma=False,
    )
```

```python
import functools

import jax
import jax.numpy as jnp
from jax import lax
from jax.experimental import pallas as pl
from jax.experimental.pallas import tpu as pltpu
from jax.sharding import PartitionSpec as P

MESH = pl.DeviceIdType.MESH
STEPS = 3
BS = 64
BLK = 1024
SLAB = 128
CH = 32
HALF = 16
OFFSETS = (0, -1, 1, 2)
ORDER = {
    "ready": (
        (),
        (78, 100, 109, 112),
        (196, 199, 221, 228),
    ),
    "direct": (
        (3, 4, 6, 7, 16, 17, 27, 28),
        (106, 107, 115, 119, 129, 126, 138, 140),
        (213, 211, 215, 214, 236, 237, 244, 245),
    ),
    "handed": (
        (10, 22, 38, 39),
        (113, 131, 134, 151),
        (223, 226, 253, 259),
    ),
    "split_p": (
        (19, 30, 42, 47),
        (116, 132, 142, 158),
        (232, 242, 260, 268),
    ),
    "split_q": (
        (50, 64, 83, 85),
        (147, 166, 186, 204),
        (250, 273, 292, 305),
    ),
    "product": (
        (51, 53, 54, 55, 65, 66, 67, 71, 92, 93, 94, 95, 86, 87, 88, 89),
        (148, 149, 150, 159, 167, 168, 169, 170, 187, 188, 189, 190, 205, 206, 207, 208),
        (251, 252, 261, 269, 276, 277, 280, 282, 293, 295, 299, 300, 306, 307, 308, 309),
    ),
    "send_out": (
        (56, 57, 72, 73, 96, 97, 91, 90),
        (160, 161, 172, 177, 191, 192, 209, 210),
        (270, 271, 283, 284, 301, 302, 310, 311),
    ),
    "add_on": (
        (68, 69, 79, 80, 103, 102, 104, 105),
        (178, 180, 182, 183, 201, 202, 217, 218),
        (288, 287, 296, 298, 313, 312, 315, 316),
    ),
    "end": (
        (77, 99, 108, 111),
        (195, 198, 220, 227),
        (314, 317, 318, 319),
    ),
    "bc": (
        (0, 2, 15, 5, 11, 25, 8, 20, 33, 23, 40, 49, 1, 9, 18, 13, 26, 37, 14, 29, 41, 35, 52, 63, 12, 24, 34, 31, 44, 82, 32, 48, 60, 58, 70, 81, 21, 36, 46, 43, 61, 75, 45, 62, 76, 59, 74, 84),
        (98, 101, 118, 114, 123, 135, 117, 128, 136, 120, 130, 143, 110, 121, 124, 122, 133, 146, 125, 141, 154, 139, 153, 165, 127, 145, 157, 144, 162, 175, 152, 171, 181, 155, 174, 184, 137, 156, 176, 163, 179, 194, 164, 193, 197, 173, 185, 203),
        (200, 212, 225, 219, 230, 240, 224, 234, 241, 229, 239, 249, 216, 222, 233, 231, 243, 256, 235, 248, 264, 246, 258, 272, 238, 254, 267, 255, 266, 285, 257, 275, 290, 263, 281, 291, 247, 262, 279, 265, 286, 297, 274, 289, 303, 278, 294, 304),
    ),
}
ROLES = (("x", "z", "y"), ("z", "y", "x"), ("y", "x", "z"))
F32 = jnp.float32
BF16 = jnp.bfloat16


def nt_dot(left, right):
    return lax.dot_general(left, right, (((1,), (1,)), ((), ())), preferred_element_type=F32)


def split(value):
    high = value.astype(BF16)
    return high, (value - high.astype(F32)).astype(BF16)


def lane_rows(i):
    unit = i // 2
    return [(2 * (i % 2) + q) * 256 + core * SLAB + unit * CH for q in (0, 1) for core in (0, 1)]


def body(
    dens, pat, br, fin_out, tr_out, pat_out,
    pbuf, qbuf, phi, plo, qcat, obuf, r1, r2, patf, gbuf, mbuf, vsend, vcore, vaxis, fin, wide,
    ag_s, ag_r, af_s, af_r, cx_s, cx_r, bc_s, bc_r, rs_s, rs_r, pt_s, pt_r, tr_s, tr_r, fx_s, fx_r,
):
    col = lax.axis_index("col")
    k = lax.axis_index("depth")
    pos = {"x": lax.axis_index("row"), "y": lax.rem(col, 4), "z": lax.div(col, 4)}
    other = 1 - k

    def wrap(value):
        return lax.rem(value + 8, 4)

    def device(x, y, z, core):
        return (x, z * 4 + y, core)

    def at(axis, delta):
        place = dict(pos)
        place[axis] = wrap(place[axis] + delta)
        return device(place["x"], place["y"], place["z"], k)

    partner = device(pos["x"], pos["y"], pos["z"], other)

    def rcopy(src, dst, send, recv, dev):
        return pltpu.make_async_remote_copy(
            src_ref=src, dst_ref=dst, send_sem=send, recv_sem=recv, device_id=dev, device_id_type=MESH
        )

    barrier = pltpu.get_barrier_semaphore()
    greet = [partner]
    for axis in ("x", "y", "z"):
        for delta in (1, -1, 2):
            greet.append(at(axis, delta))
    for i in range(4):
        greet.append(device(pos["y"], i, pos["z"], other))
        greet.append(device(pos["x"], i, pos["y"], other))
    for dev in greet:
        pl.semaphore_signal(barrier, inc=1, device_id=dev, device_id_type=MESH)

    for i in range(8):
        mine = pl.ds(pl.multiple_of(k * 128, 128), 128)
        piece = jnp.concatenate([dens[row:row + CH, mine] for row in lane_rows(i)], axis=0)
        pbuf[0, pos["y"], k, :, i * 128:(i + 1) * 128] = piece.T
    vsend[0] = jnp.zeros((8, 128), F32)
    wide[...] = jnp.zeros_like(wide)
    wide[0:4, 0:16] = pat[...].astype(F32)
    patf[...] = wide[...].T[0:16, :]
    pl.semaphore_wait(barrier, len(greet))

    def pattern_copies():
        found = []
        for i in range(4):
            found.append(rcopy(patf, gbuf.at[0, pos["y"]], pt_s.at[0, i], pt_r.at[0, pos["y"]],
                               device(i, pos["x"], pos["z"], other)))
            found.append(rcopy(patf, gbuf.at[1, pos["y"]], pt_s.at[1, i], pt_r.at[1, pos["y"]],
                               device(pos["x"], pos["z"], i, other)))
        return found

    def pattern_wait(s):
        for i in range(4):
            rcopy(patf, gbuf.at[s, i], pt_s.at[s, i], pt_r.at[s, i], partner).wait_recv()

    def square_sum(s, slab):
        total = jnp.zeros((1, BLK), F32)
        for i in range(4):
            part = pbuf[s, slab, k, i * CH:(i + 1) * CH, :]
            total = total + jnp.sum(part * part, axis=0, keepdims=True)
        vsend[0, s:s + 1, :] = jnp.broadcast_to(jnp.sum(total, axis=1, keepdims=True), (1, 128))

    def trace_core():
        return rcopy(vsend.at[0], vcore, tr_s.at[0, 0], tr_r.at[0, 0], partner)

    def trace_core_end():
        trace_core().wait()
        vsend[1] = vsend[0] + vcore[...]

    def trace_axis_copies(stage, axis):
        me = pos[axis]
        return [
            rcopy(vsend.at[stage], vaxis.at[stage, me], tr_s.at[stage, d], tr_r.at[stage, me], at(axis, d))
            for d in (1, 2, 3)
        ]

    def trace_axis_start(stage, axis):
        for copy in trace_axis_copies(stage, axis):
            copy.start()
        vaxis[stage, pos[axis]] = vsend[stage]

    def trace_axis_end(stage, axis):
        for d in (1, 2, 3):
            src = wrap(pos[axis] + d)
            rcopy(vsend.at[stage], vaxis.at[stage, src], tr_s.at[stage, d], tr_r.at[stage, src], partner).wait_recv()
        for copy in trace_axis_copies(stage, axis):
            copy.wait_send()
        vsend[stage + 1] = (vaxis[stage, 0] + vaxis[stage, 1]) + (vaxis[stage, 2] + vaxis[stage, 3])

    def fin_copy(j, core):
        ref = fin.at[core, pl.ds(j * CH, CH)]
        return rcopy(ref, ref, fx_s.at[j], fx_r.at[j], partner)

    def make_step(s):
        step = {}
        an, bn, cn = ROLES[s]
        a, b, c = pos[an], pos[bn], pos[cn]
        d = wrap(b - c)
        root = d == 0
        up, down, far = wrap(a + 1), wrap(a - 1), wrap(a + 2)

        def rows(j):
            return pl.ds(j * CH, CH)

        def half_rows(j, direction):
            return pl.ds(j * CH + direction * HALF, HALF)

        def sign(direction):
            return 1 - 2 * direction

        def ag_copy(direction, j):
            ref = pbuf.at[s, c, k, rows(j)]
            return rcopy(ref, ref, ag_s.at[s, direction, j], ag_r.at[s, direction, j], at(cn, sign(direction)))

        def ag_wait(direction, j):
            ref = pbuf.at[s, wrap(c - sign(direction)), k, rows(j)]
            rcopy(ref, ref, ag_s.at[s, direction, j], ag_r.at[s, direction, j], partner).wait_recv()

        def af_copy(direction, j):
            ref = pbuf.at[s, wrap(c - sign(direction)), k, half_rows(j, direction)]
            return rcopy(ref, ref, af_s.at[s, direction, j], af_r.at[s, direction, j], at(cn, sign(direction)))

        def af_wait(direction, j):
            ref = pbuf.at[s, wrap(c + 2), k, half_rows(j, direction)]
            rcopy(ref, ref, af_s.at[s, direction, j], af_r.at[s, direction, j], partner).wait_recv()

        def cx_copy(j, i):
            ref = pbuf.at[s, wrap(c + OFFSETS[i]), k, rows(j)]
            return rcopy(ref, ref, cx_s.at[s, j, i], cx_r.at[s, j, i], partner)

        def cx_wait(j, i):
            ref = pbuf.at[s, wrap(c + OFFSETS[i]), other, rows(j)]
            rcopy(ref, ref, cx_s.at[s, j, i], cx_r.at[s, j, i], partner).wait_recv()

        def bc_copy(direction, j, i, from_root):
            q = wrap(c + OFFSETS[i])
            place = half_rows(j, direction)
            dst = qbuf.at[s, q, place]
            src = pbuf.at[s, q, k, place] if from_root else dst
            return rcopy(src, dst, bc_s.at[s, direction, j, i], bc_r.at[s, direction, j, i], at(bn, sign(direction)))

        def bc_root(j, *parts):
            @pl.when(root)
            def _():
                for i in parts:
                    bc_copy(0, j, i, True).start()
                    bc_copy(1, j, i, True).start()

        def bc_hop(hop, j, i):
            def hand_on(*directions):
                for direction in directions:
                    copy = bc_copy(direction, j, i, False)
                    copy.wait_recv()
                    if hop < 3:
                        copy.start()

            if hop == 2:
                pl.when(d == 2)(functools.partial(hand_on, 0, 1))
            else:
                pl.when(d == hop)(functools.partial(hand_on, 0))
                pl.when(d == 4 - hop)(functools.partial(hand_on, 1))

        def ready(j):
            ag_copy(0, j).start()
            ag_copy(1, j).start()
            bc_root(j, 0)
            cx_copy(j, 0).start()

        def direct(j, direction):
            ag_wait(direction, j)
            af_copy(direction, j).start()
            if s == 0 and j < 2 and direction == 1:
                ready(j + 2)
            cx_copy(j, 1 + direction).start()
            bc_root(j, 1 + direction)

        def handed(j):
            for direction in (0, 1):
                af_wait(direction, j)
            cx_copy(j, 3).start()
            bc_root(j, 3)

        def split_p(j):
            for i in range(4):
                cx_wait(j, i)

            @pl.loop(0, 8)
            def _(i):
                row = pl.multiple_of(j * 8 * CH + i * CH, CH)
                high, low = split(pbuf[s, lax.div(i, 2), lax.rem(i, 2), rows(j)])
                phi[s % 2, pl.ds(row, CH), :] = high
                plo[s % 2, pl.ds(row, CH), :] = low

        def split_q(j):
            def halves(read):
                for q in range(4):
                    high, low = split(read(q))
                    qcat[j, q * CH:(q + 1) * CH, :] = high
                    qcat[j, SLAB + q * CH:SLAB + (q + 1) * CH, :] = low

            @pl.when(root)
            def _():
                halves(lambda q: pbuf[s, q, k, rows(j)])

            @pl.when(jnp.logical_not(root))
            def _():
                halves(lambda q: qbuf[s, q, rows(j)])

        def product(j, first, last):
            weight = br[s].astype(F32)
            scale = 1.0 - 2.0 * weight
            linear = 2.0 * weight * (a == b).astype(F32)

            @pl.loop(first, last)
            def _(n):
                lanes = pl.ds(pl.multiple_of(n * 256, 256), 256)
                both = nt_dot(qcat[j], phi[s % 2, lanes, :])
                value = both[:SLAB] + both[SLAB:] + nt_dot(qcat[j, :SLAB, :], plo[s % 2, lanes, :])
                same = qcat[j, :SLAB, lanes].astype(F32) + qcat[j, SLAB:, lanes].astype(F32)
                obuf[s, j, :, lanes] = scale * value + linear * same

        def send_out(j, i):
            for direction in (0, 1):
                rs_copy(direction, i, j).start()

        def out_half(q, second):
            return pl.ds(pl.multiple_of(q * CH + second * HALF, HALF), HALF)

        def rs_copy(direction, i, j):
            near = up if direction == 0 else down
            if i == 0:
                src, dst = obuf.at[s, j, out_half(far, direction)], r1.at[s, direction, j]
            else:
                second = 1 - direction if i == 1 else direction
                src = obuf.at[s, j, out_half(near, second)]
                dst = r2.at[s, direction, j, pl.ds(second * HALF, HALF)]
            return rcopy(src, dst, rs_s.at[s, direction, j, i], rs_r.at[s, direction, j, i], at(an, sign(direction)))

        def add_on(j, direction):
            rs_copy(direction, 0, j).wait_recv()
            place = out_half(up if direction == 0 else down, direction)
            obuf[s, j, place, :] = obuf[s, j, place, :] + r1[s, direction, j]
            rs_copy(direction, 2, j).start()

        def mask():
            pattern_wait(s)
            line = lax.broadcasted_iota(jnp.int32, (SLAB, 16), 0)
            block = lax.broadcasted_iota(jnp.int32, (SLAB, 16), 1)
            pick = (block == a * 4 + k * 2 + line // BS).astype(F32)
            left = lax.broadcasted_iota(jnp.int32, (128, 256), 0)
            right = lax.broadcasted_iota(jnp.int32, (128, 256), 1)
            chosen = [jnp.dot(pick, gbuf[s, q], preferred_element_type=F32) for q in range(4)]
            for pair in range(2):
                value = jnp.zeros((SLAB, 256), F32)
                for q in range(4):
                    wanted = (right % 64) // CH * 2 + pair
                    spread = jnp.logical_and(right // 64 == q, left == wanted).astype(F32)
                    value = value + jnp.dot(chosen[q], spread, preferred_element_type=F32)
                for i in (2 * pair, 2 * pair + 1):
                    mbuf[s, :, i * 256:(i + 1) * 256] = value

        def finish(j):
            for i in (1, 2):
                for direction in (0, 1):
                    rs_copy(direction, i, j).wait_recv()
            place = pl.ds(pl.multiple_of(a * CH, CH), CH)
            value = obuf[s, j, place, :] + (r2[s, 0, j] + r2[s, 1, j])
            if s < 2:
                pbuf[s + 1, a, k, rows(j), :] = value * mbuf[s, rows(j), :]
            else:
                fin[k, rows(j), :] = value
                fin_copy(j, k).start()

        def sent():
            for direction in (0, 1):
                for j in range(4):
                    ag_copy(direction, j).wait_send()
                    af_copy(direction, j).wait_send()

                @pl.when(d != (3 if direction == 0 else 1))
                def _():
                    for j in range(4):
                        for i in range(4):
                            bc_copy(direction, j, i, False).wait_send()
            for j in range(4):
                for i in range(4):
                    cx_copy(j, i).wait_send()
            if s == 0:
                for copy in pattern_copies():
                    copy.wait_send()

        def rs_sent():
            for direction in (0, 1):
                for j in range(4):
                    for i in range(3):
                        rs_copy(direction, i, j).wait_send()

        step.update(locals())
        return step

    steps = [make_step(s) for s in range(STEPS)]
    steps[0]["ready"](0)
    steps[0]["ready"](1)
    for copy in pattern_copies():
        copy.start()

    events = {}

    def due(name, time, act, needs=()):
        time = max([time] + [events[need][0] for need in needs])
        events[name] = (time, len(events), act)

    call = functools.partial
    units = range(4)
    hops = (1, 2, 3)
    for s in range(STEPS):
        now = steps[s]

        def place(kind, n):
            return ORDER[kind][s][n]

        for j in units:
            begun = [("direct", 0, j - 2, 1)] if j > 1 else []
            if s:
                due(("ready", s, j), place("ready", j), call(now["ready"], j), [("end", s - 1, j)])
                begun = [("ready", s, j)]
            for n in (0, 1):
                due(("direct", s, j, n), place("direct", 2 * j + n), call(now["direct"], j, n), begun)
            due(("handed", s, j), place("handed", j), call(now["handed"], j), [("direct", s, j, 0), ("direct", s, j, 1)])
            due(("split_p", s, j), place("split_p", j), call(now["split_p"], j), [("handed", s, j)])
            starts = (begun, [("direct", s, j, 0)], [("direct", s, j, 1)], [("handed", s, j)])
            for i in units:
                for hop in hops:
                    needs = [("bc", s, j, i, hop - 1)] if hop > 1 else starts[i]
                    due(("bc", s, j, i, hop), place("bc", j * 12 + i * 3 + hop - 1), call(now["bc_hop"], hop, j, i), needs)
        if s < 2:
            due(("mask", s), place("direct", 7), now["mask"], [("direct", s, 3, 1)])
        for j in units:
            due(("split_q", s, j), place("split_q", j), call(now["split_q"], j),
                [("bc", s, j, i, hop) for i in units for hop in hops] + [("handed", s, j)])
            before = ("split_q", s, j)
            for n in units:
                due(("product", s, j, n), place("product", j * 4 + n), call(now["product"], j, n, n + 1),
                    [before, ("split_p", s, n)])
                before = ("product", s, j, n)
            for n in (0, 1):
                due(("send_out", s, j, n), place("send_out", 2 * j + n), call(now["send_out"], j, n), [before])
            for n in (0, 1):
                due(("add_on", s, j, n), place("add_on", 2 * j + n), call(now["add_on"], j, n), [("send_out", s, j, 0)])
            due(("end", s, j), place("end", j), call(now["finish"], j),
                [("add_on", s, j, 0), ("add_on", s, j, 1), ("send_out", s, j, 1)] + ([("mask", s)] if s < 2 else []))
        late = [("end", s - 1, n) for n in units] if s else []
        due(("sum", s), place("direct", 5), call(square_sum, s, now["c"]), late)
        if s > 0:
            due(("sent", s - 1), place("handed", 2), steps[s - 1]["sent"], late + [("direct", s, 3, 0), ("direct", s, 3, 1)])
            due(("rs_sent", s - 1), place("handed", 3), steps[s - 1]["rs_sent"], late + [("direct", s, 3, 0), ("direct", s, 3, 1)])
        if s == 2:
            chain = [
                (place("direct", 5), lambda: trace_core().start()),
                (place("handed", 2), trace_core_end), (place("handed", 2), call(trace_axis_start, 1, "x")),
                (place("split_p", 3), call(trace_axis_end, 1, "x")), (place("split_p", 3), call(trace_axis_start, 2, "y")),
                (place("send_out", 5), call(trace_axis_end, 2, "y")), (place("send_out", 5), call(trace_axis_start, 3, "z")),
                (place("add_on", 7), call(trace_axis_end, 3, "z")),
            ]
            before = ("sum", 2)
            for n, (time, act) in enumerate(chain):
                due(("trace", n), time, act, [before])
                before = ("trace", n)
            due(("sent", s), place("add_on", 7), now["sent"], [("split_q", s, j) for j in units])
    for _, _, act in sorted(events.values(), key=lambda event: event[:2]):
        act()
    tr_out[...] = vsend[4]
    pat_out[...] = patf[...]
    steps[2]["rs_sent"]()
    for j in range(4):
        fin_copy(j, other).wait_recv()
    for j in range(4):
        fin_copy(j, k).wait_send()
    fin_out[...] = fin[...]


def place_body(fin, pat, totals, out, traces):
    left = lax.broadcasted_iota(jnp.int32, (128, 256), 0)
    right = lax.broadcasted_iota(jnp.int32, (128, 256), 1)
    spread = (left == right // BS).astype(F32)
    line = lax.broadcasted_iota(jnp.int32, (128, 16), 0)
    block = lax.broadcasted_iota(jnp.int32, (128, 16), 1)
    for i in range(8):
        here = [line // CH == n for n in range(4)]
        wanted = sum(jnp.where(here[n], row // BS, 0) for n, row in enumerate(lane_rows(i)))
        pick = (block == wanted).astype(F32)
        chosen = jnp.dot(pick, pat[...], preferred_element_type=F32)
        mask = jnp.dot(chosen, spread, preferred_element_type=F32)
        for half in range(2):
            lanes = slice(half * 128, (half + 1) * 128)
            part = fin[half, :, i * 128:(i + 1) * 128].T * mask[:, lanes]
            for n, row in enumerate(lane_rows(i)):
                out[row:row + CH, lanes] = part[n * CH:(n + 1) * CH]
    for i in range(STEPS):
        traces[i] = totals[i, 0]


def per_device(density, pattern, branches):
    vmem = pl.BlockSpec(memory_space=pltpu.VMEM)
    dma = pltpu.SemaphoreType.DMA
    last, totals, kept = pl.pallas_call(
        body,
        out_shape=(
            jax.ShapeDtypeStruct((2, SLAB, BLK), F32),
            jax.ShapeDtypeStruct((8, 128), F32),
            jax.ShapeDtypeStruct((16, 128), F32),
        ),
        in_specs=[vmem, vmem, pl.BlockSpec(memory_space=pltpu.SMEM)],
        out_specs=(vmem, vmem, vmem),
        scratch_shapes=[
            pltpu.VMEM((STEPS, 4, 2, SLAB, BLK), F32),
            pltpu.VMEM((STEPS, 4, SLAB, BLK), F32),
            pltpu.VMEM((2, BLK, BLK), BF16),
            pltpu.VMEM((2, BLK, BLK), BF16),
            pltpu.VMEM((4, 2 * SLAB, BLK), BF16),
            pltpu.VMEM((STEPS, 4, SLAB, BLK), F32),
            pltpu.VMEM((STEPS, 2, 4, HALF, BLK), F32),
            pltpu.VMEM((STEPS, 2, 4, CH, BLK), F32),
            pltpu.VMEM((16, 128), F32),
            pltpu.VMEM((2, 4, 16, 128), F32),
            pltpu.VMEM((2, SLAB, BLK), F32),
            pltpu.VMEM((5, 8, 128), F32),
            pltpu.VMEM((8, 128), F32),
            pltpu.VMEM((4, 4, 8, 128), F32),
            pltpu.VMEM((2, SLAB, BLK), F32),
            pltpu.VMEM((128, 128), F32),
            dma((STEPS, 2, 4)), dma((STEPS, 2, 4)),
            dma((STEPS, 2, 4)), dma((STEPS, 2, 4)),
            dma((STEPS, 4, 4)), dma((STEPS, 4, 4)),
            dma((STEPS, 2, 4, 4)), dma((STEPS, 2, 4, 4)),
            dma((STEPS, 2, 4, 3)), dma((STEPS, 2, 4, 3)),
            dma((2, 4)), dma((2, 4)),
            dma((4, 4)), dma((4, 4)),
            dma((4,)), dma((4,)),
        ],
        compiler_params=pltpu.CompilerParams(
            collective_id=0, has_side_effects=True, vmem_limit_bytes=56 * 2**20
        ),
        name="purify",
    )(density, pattern.T, branches)
    smem = pl.BlockSpec(memory_space=pltpu.SMEM)
    return pl.pallas_call(
        place_body,
        out_shape=(jax.ShapeDtypeStruct((BLK, 256), F32), jax.ShapeDtypeStruct((STEPS,), F32)),
        in_specs=[vmem, vmem, smem],
        out_specs=(vmem, smem),
        name="place",
    )(last, kept, totals)


def solution(mesh):
    return jax.shard_map(
        per_device,
        mesh=mesh,
        in_specs=(P("row", "col"), P("row", "col"), P()),
        out_specs=(P("row", "col"), P()),
        check_vma=False,
    )
```

```python
import functools

import jax
import jax.numpy as jnp
from jax import lax
from jax.experimental import pallas as pl
from jax.experimental.pallas import tpu as pltpu
from jax.sharding import PartitionSpec as P

MESH = pl.DeviceIdType.MESH
STEPS = 3
BS = 64
BLK = 1024
SLAB = 128
CH = 32
HALF = 16
OFFSETS = (0, -1, 1, 2)
ORDER = {
    "ready": (
        (),
        (78, 100, 109, 112),
        (196, 199, 221, 228),
    ),
    "direct": (
        (3, 4, 6, 7, 16, 17, 27, 28),
        (106, 107, 115, 119, 129, 126, 138, 140),
        (213, 211, 215, 214, 236, 237, 244, 245),
    ),
    "handed": (
        (10, 22, 38, 39),
        (113, 131, 134, 151),
        (223, 226, 253, 259),
    ),
    "split_p": (
        (19, 30, 42, 47),
        (116, 132, 142, 158),
        (232, 242, 260, 268),
    ),
    "split_q": (
        (50, 64, 83, 85),
        (147, 166, 186, 204),
        (250, 273, 292, 305),
    ),
    "product": (
        (51, 53, 54, 55, 65, 66, 67, 71, 92, 93, 94, 95, 86, 87, 88, 89),
        (148, 149, 150, 159, 167, 168, 169, 170, 187, 188, 189, 190, 205, 206, 207, 208),
        (251, 252, 261, 269, 276, 277, 280, 282, 293, 295, 299, 300, 306, 307, 308, 309),
    ),
    "send_out": (
        (56, 57, 72, 73, 96, 97, 91, 90),
        (160, 161, 172, 177, 191, 192, 209, 210),
        (270, 271, 283, 284, 301, 302, 310, 311),
    ),
    "add_on": (
        (68, 69, 79, 80, 103, 102, 104, 105),
        (178, 180, 182, 183, 201, 202, 217, 218),
        (288, 287, 296, 298, 313, 312, 315, 316),
    ),
    "end": (
        (77, 99, 108, 111),
        (195, 198, 220, 227),
        (314, 317, 318, 319),
    ),
    "bc": (
        (0, 2, 15, 5, 11, 25, 8, 20, 33, 23, 40, 49, 1, 9, 18, 13, 26, 37, 14, 29, 41, 35, 52, 63, 12, 24, 34, 31, 44, 82, 32, 48, 60, 58, 70, 81, 21, 36, 46, 43, 61, 75, 45, 62, 76, 59, 74, 84),
        (98, 101, 118, 114, 123, 135, 117, 128, 136, 120, 130, 143, 110, 121, 124, 122, 133, 146, 125, 141, 154, 139, 153, 165, 127, 145, 157, 144, 162, 175, 152, 171, 181, 155, 174, 184, 137, 156, 176, 163, 179, 194, 164, 193, 197, 173, 185, 203),
        (200, 212, 225, 219, 230, 240, 224, 234, 241, 229, 239, 249, 216, 222, 233, 231, 243, 256, 235, 248, 264, 246, 258, 272, 238, 254, 267, 255, 266, 285, 257, 275, 290, 263, 281, 291, 247, 262, 279, 265, 286, 297, 274, 289, 303, 278, 294, 304),
    ),
}
ROLES = (("x", "z", "y"), ("z", "y", "x"), ("y", "x", "z"))
F32 = jnp.float32
BF16 = jnp.bfloat16


def nt_dot(left, right):
    return lax.dot_general(left, right, (((1,), (1,)), ((), ())), preferred_element_type=F32)


def split(value):
    high = value.astype(BF16)
    return high, (value - high.astype(F32)).astype(BF16)


def lane_rows(i):
    unit = i // 2
    return [(2 * (i % 2) + q) * 256 + core * SLAB + unit * CH for q in (0, 1) for core in (0, 1)]


def body(
    dens, pat, br, fin_out, tr_out, pat_out,
    pbuf, qbuf, phi, plo, qcat, obuf, r1, r2, patf, gbuf, mbuf, vsend, vcore, vaxis, fin, wide,
    ag_s, ag_r, af_r, cx_s, cx_r, bc_s, bc_r, rs_s, rs_r, pt_s, pt_r, tr_s, tr_r, fx_s, fx_r,
):
    col = lax.axis_index("col")
    k = lax.axis_index("depth")
    pos = {"x": lax.axis_index("row"), "y": lax.rem(col, 4), "z": lax.div(col, 4)}
    other = 1 - k

    def wrap(value):
        return lax.rem(value + 8, 4)

    def device(x, y, z, core):
        return (x, z * 4 + y, core)

    def at(axis, delta):
        place = dict(pos)
        place[axis] = wrap(place[axis] + delta)
        return device(place["x"], place["y"], place["z"], k)

    partner = device(pos["x"], pos["y"], pos["z"], other)

    def rcopy(src, dst, send, recv, dev):
        return pltpu.make_async_remote_copy(
            src_ref=src, dst_ref=dst, send_sem=send, recv_sem=recv, device_id=dev, device_id_type=MESH
        )

    barrier = pltpu.get_barrier_semaphore()
    greet = [partner]
    for axis in ("x", "y", "z"):
        for delta in (1, -1, 2):
            greet.append(at(axis, delta))
    for i in range(4):
        greet.append(device(pos["y"], i, pos["z"], other))
        greet.append(device(pos["x"], i, pos["y"], other))
    for dev in greet:
        pl.semaphore_signal(barrier, inc=1, device_id=dev, device_id_type=MESH)

    for i in range(8):
        mine = pl.ds(pl.multiple_of(k * 128, 128), 128)
        piece = jnp.concatenate([dens[row:row + CH, mine] for row in lane_rows(i)], axis=0)
        pbuf[0, pos["y"], k, :, i * 128:(i + 1) * 128] = piece.T
    vsend[0] = jnp.zeros((8, 128), F32)
    wide[...] = jnp.zeros_like(wide)
    wide[0:4, 0:16] = pat[...].astype(F32)
    patf[...] = wide[...].T[0:16, :]
    pl.semaphore_wait(barrier, len(greet))

    def pattern_copies():
        found = []
        for i in range(4):
            found.append(rcopy(patf, gbuf.at[0, pos["y"]], pt_s.at[0, i], pt_r.at[0, pos["y"]],
                               device(i, pos["x"], pos["z"], other)))
            found.append(rcopy(patf, gbuf.at[1, pos["y"]], pt_s.at[1, i], pt_r.at[1, pos["y"]],
                               device(pos["x"], pos["z"], i, other)))
        return found

    def pattern_wait(s):
        for i in range(4):
            rcopy(patf, gbuf.at[s, i], pt_s.at[s, i], pt_r.at[s, i], partner).wait_recv()

    def square_sum(s, slab):
        total = jnp.zeros((1, BLK), F32)
        for i in range(4):
            part = pbuf[s, slab, k, i * CH:(i + 1) * CH, :]
            total = total + jnp.sum(part * part, axis=0, keepdims=True)
        vsend[0, s:s + 1, :] = jnp.broadcast_to(jnp.sum(total, axis=1, keepdims=True), (1, 128))

    def trace_core():
        return rcopy(vsend.at[0], vcore, tr_s.at[0, 0], tr_r.at[0, 0], partner)

    def trace_core_end():
        trace_core().wait()
        vsend[1] = vsend[0] + vcore[...]

    def trace_axis_copies(stage, axis):
        me = pos[axis]
        return [
            rcopy(vsend.at[stage], vaxis.at[stage, me], tr_s.at[stage, d], tr_r.at[stage, me], at(axis, d))
            for d in (1, 2, 3)
        ]

    def trace_axis_start(stage, axis):
        for copy in trace_axis_copies(stage, axis):
            copy.start()
        vaxis[stage, pos[axis]] = vsend[stage]

    def trace_axis_end(stage, axis):
        for d in (1, 2, 3):
            src = wrap(pos[axis] + d)
            rcopy(vsend.at[stage], vaxis.at[stage, src], tr_s.at[stage, d], tr_r.at[stage, src], partner).wait_recv()
        for copy in trace_axis_copies(stage, axis):
            copy.wait_send()
        vsend[stage + 1] = (vaxis[stage, 0] + vaxis[stage, 1]) + (vaxis[stage, 2] + vaxis[stage, 3])

    def fin_copy(j, core):
        ref = fin.at[core, pl.ds(j * CH, CH)]
        return rcopy(ref, ref, fx_s.at[j], fx_r.at[j], partner)

    def make_step(s):
        step = {}
        an, bn, cn = ROLES[s]
        a, b, c = pos[an], pos[bn], pos[cn]
        d = wrap(b - c)
        root = d == 0
        up, down, far = wrap(a + 1), wrap(a - 1), wrap(a + 2)

        def rows(j):
            return pl.ds(j * CH, CH)

        def half_rows(j, direction):
            return pl.ds(j * CH + direction * HALF, HALF)

        def sign(direction):
            return 1 - 2 * direction

        def ag_copy(direction, j):
            ref = pbuf.at[s, c, k, rows(j)]
            return rcopy(ref, ref, ag_s.at[s, direction], ag_r.at[s, direction, j], at(cn, sign(direction)))

        def ag_wait(direction, j):
            ref = pbuf.at[s, wrap(c - sign(direction)), k, rows(j)]
            rcopy(ref, ref, ag_s.at[s, direction], ag_r.at[s, direction, j], partner).wait_recv()

        def af_copy(direction, j):
            ref = pbuf.at[s, wrap(c - sign(direction)), k, half_rows(j, direction)]
            return rcopy(ref, ref, ag_s.at[s, direction], af_r.at[s, direction, j], at(cn, sign(direction)))

        def af_wait(direction, j):
            ref = pbuf.at[s, wrap(c + 2), k, half_rows(j, direction)]
            rcopy(ref, ref, ag_s.at[s, direction], af_r.at[s, direction, j], partner).wait_recv()

        def cx_copy(j, i):
            ref = pbuf.at[s, wrap(c + OFFSETS[i]), k, rows(j)]
            return rcopy(ref, ref, cx_s.at[s], cx_r.at[s, j, i], partner)

        def cx_wait(j, i):
            ref = pbuf.at[s, wrap(c + OFFSETS[i]), other, rows(j)]
            rcopy(ref, ref, cx_s.at[s], cx_r.at[s, j, i], partner).wait_recv()

        def bc_copy(direction, j, i, from_root):
            q = wrap(c + OFFSETS[i])
            place = half_rows(j, direction)
            dst = qbuf.at[s, q, place]
            src = pbuf.at[s, q, k, place] if from_root else dst
            return rcopy(src, dst, bc_s.at[s, direction], bc_r.at[s, direction, j, i], at(bn, sign(direction)))

        def bc_root(j, *parts):
            @pl.when(root)
            def _():
                for i in parts:
                    bc_copy(0, j, i, True).start()
                    bc_copy(1, j, i, True).start()

        def bc_hop(hop, j, i):
            def hand_on(*directions):
                for direction in directions:
                    copy = bc_copy(direction, j, i, False)
                    copy.wait_recv()
                    if hop < 3:
                        copy.start()

            if hop == 2:
                pl.when(d == 2)(functools.partial(hand_on, 0, 1))
            else:
                pl.when(d == hop)(functools.partial(hand_on, 0))
                pl.when(d == 4 - hop)(functools.partial(hand_on, 1))

        def ready(j):
            ag_copy(0, j).start()
            ag_copy(1, j).start()
            bc_root(j, 0)
            cx_copy(j, 0).start()

        def direct(j, direction):
            ag_wait(direction, j)
            af_copy(direction, j).start()
            if s == 0 and j < 2 and direction == 1:
                ready(j + 2)
            cx_copy(j, 1 + direction).start()
            bc_root(j, 1 + direction)

        def handed(j):
            for direction in (0, 1):
                af_wait(direction, j)
            cx_copy(j, 3).start()
            bc_root(j, 3)

        def split_p(j):
            for i in range(4):
                cx_wait(j, i)

            @pl.loop(0, 8)
            def _(i):
                row = pl.multiple_of(j * 8 * CH + i * CH, CH)
                high, low = split(pbuf[s, lax.div(i, 2), lax.rem(i, 2), rows(j)])
                phi[s % 2, pl.ds(row, CH), :] = high
                plo[s % 2, pl.ds(row, CH), :] = low

        def split_q(j):
            def halves(read):
                for q in range(4):
                    high, low = split(read(q))
                    qcat[j, q * CH:(q + 1) * CH, :] = high
                    qcat[j, SLAB + q * CH:SLAB + (q + 1) * CH, :] = low

            @pl.when(root)
            def _():
                halves(lambda q: pbuf[s, q, k, rows(j)])

            @pl.when(jnp.logical_not(root))
            def _():
                halves(lambda q: qbuf[s, q, rows(j)])

        def product(j, first, last):
            weight = br[s].astype(F32)
            scale = 1.0 - 2.0 * weight
            linear = 2.0 * weight * (a == b).astype(F32)

            @pl.loop(first, last)
            def _(n):
                lanes = pl.ds(pl.multiple_of(n * 256, 256), 256)
                both = nt_dot(qcat[j], phi[s % 2, lanes, :])
                value = both[:SLAB] + both[SLAB:] + nt_dot(qcat[j, :SLAB, :], plo[s % 2, lanes, :])
                same = qcat[j, :SLAB, lanes].astype(F32) + qcat[j, SLAB:, lanes].astype(F32)
                obuf[s, j, :, lanes] = scale * value + linear * same

        def send_out(j, i):
            for direction in (0, 1):
                rs_copy(direction, i, j).start()

        def out_half(q, second):
            return pl.ds(pl.multiple_of(q * CH + second * HALF, HALF), HALF)

        def rs_copy(direction, i, j):
            near = up if direction == 0 else down
            if i == 0:
                src, dst = obuf.at[s, j, out_half(far, direction)], r1.at[s, direction, j]
            else:
                second = 1 - direction if i == 1 else direction
                src = obuf.at[s, j, out_half(near, second)]
                dst = r2.at[s, direction, j, pl.ds(second * HALF, HALF)]
            return rcopy(src, dst, rs_s.at[s, direction], rs_r.at[s, direction, j, i], at(an, sign(direction)))

        def add_on(j, direction):
            rs_copy(direction, 0, j).wait_recv()
            place = out_half(up if direction == 0 else down, direction)
            obuf[s, j, place, :] = obuf[s, j, place, :] + r1[s, direction, j]
            rs_copy(direction, 2, j).start()

        def mask():
            pattern_wait(s)
            line = lax.broadcasted_iota(jnp.int32, (SLAB, 16), 0)
            block = lax.broadcasted_iota(jnp.int32, (SLAB, 16), 1)
            pick = (block == a * 4 + k * 2 + line // BS).astype(F32)
            left = lax.broadcasted_iota(jnp.int32, (128, 256), 0)
            right = lax.broadcasted_iota(jnp.int32, (128, 256), 1)
            chosen = [jnp.dot(pick, gbuf[s, q], preferred_element_type=F32) for q in range(4)]
            for pair in range(2):
                value = jnp.zeros((SLAB, 256), F32)
                for q in range(4):
                    wanted = (right % 64) // CH * 2 + pair
                    spread = jnp.logical_and(right // 64 == q, left == wanted).astype(F32)
                    value = value + jnp.dot(chosen[q], spread, preferred_element_type=F32)
                for i in (2 * pair, 2 * pair + 1):
                    mbuf[s, :, i * 256:(i + 1) * 256] = value

        def finish(j):
            for i in (1, 2):
                for direction in (0, 1):
                    rs_copy(direction, i, j).wait_recv()
            place = pl.ds(pl.multiple_of(a * CH, CH), CH)
            value = obuf[s, j, place, :] + (r2[s, 0, j] + r2[s, 1, j])
            if s < 2:
                pbuf[s + 1, a, k, rows(j), :] = value * mbuf[s, rows(j), :]
            else:
                fin[k, rows(j), :] = value
                fin_copy(j, k).start()

        def all_sent(ref, send, recv):
            rcopy(ref, ref, send, recv, partner).wait_send()

        def sent():
            for direction in (0, 1):
                all_sent(pbuf.at[s, 0, :, pl.ds(0, 96)], ag_s.at[s, direction], ag_r.at[s, direction, 0])

                @pl.when(d != (3 if direction == 0 else 1))
                def _():
                    all_sent(qbuf.at[s, pl.ds(0, 2)], bc_s.at[s, direction], bc_r.at[s, direction, 0, 0])
            all_sent(qbuf.at[s], cx_s.at[s], cx_r.at[s, 0, 0])
            if s == 0:
                for copy in pattern_copies():
                    copy.wait_send()

        def rs_sent():
            for direction in (0, 1):
                all_sent(obuf.at[s, pl.ds(0, 2), pl.ds(0, 96)], rs_s.at[s, direction], rs_r.at[s, direction, 0, 0])

        step.update(locals())
        return step

    steps = [make_step(s) for s in range(STEPS)]
    steps[0]["ready"](0)
    steps[0]["ready"](1)
    for copy in pattern_copies():
        copy.start()

    events = {}

    def due(name, time, act, needs=()):
        time = max([time] + [events[need][0] for need in needs])
        events[name] = (time, len(events), act)

    call = functools.partial
    units = range(4)
    hops = (1, 2, 3)
    for s in range(STEPS):
        now = steps[s]

        def place(kind, n):
            return ORDER[kind][s][n]

        for j in units:
            begun = [("direct", 0, j - 2, 1)] if j > 1 else []
            if s:
                due(("ready", s, j), place("ready", j), call(now["ready"], j), [("end", s - 1, j)])
                begun = [("ready", s, j)]
            for n in (0, 1):
                due(("direct", s, j, n), place("direct", 2 * j + n), call(now["direct"], j, n), begun)
            due(("handed", s, j), place("handed", j), call(now["handed"], j), [("direct", s, j, 0), ("direct", s, j, 1)])
            due(("split_p", s, j), place("split_p", j), call(now["split_p"], j), [("handed", s, j)])
            starts = (begun, [("direct", s, j, 0)], [("direct", s, j, 1)], [("handed", s, j)])
            for i in units:
                for hop in hops:
                    needs = [("bc", s, j, i, hop - 1)] if hop > 1 else starts[i]
                    due(("bc", s, j, i, hop), place("bc", j * 12 + i * 3 + hop - 1), call(now["bc_hop"], hop, j, i), needs)
        if s < 2:
            due(("mask", s), place("direct", 7), now["mask"], [("direct", s, 3, 1)])
        for j in units:
            due(("split_q", s, j), place("split_q", j), call(now["split_q"], j),
                [("bc", s, j, i, hop) for i in units for hop in hops] + [("handed", s, j)])
            before = ("split_q", s, j)
            for n in units:
                due(("product", s, j, n), place("product", j * 4 + n), call(now["product"], j, n, n + 1),
                    [before, ("split_p", s, n)])
                before = ("product", s, j, n)
            for n in (0, 1):
                due(("send_out", s, j, n), place("send_out", 2 * j + n), call(now["send_out"], j, n), [before])
            for n in (0, 1):
                due(("add_on", s, j, n), place("add_on", 2 * j + n), call(now["add_on"], j, n), [("send_out", s, j, 0)])
            due(("end", s, j), place("end", j), call(now["finish"], j),
                [("add_on", s, j, 0), ("add_on", s, j, 1), ("send_out", s, j, 1)] + ([("mask", s)] if s < 2 else []))
        late = [("end", s - 1, n) for n in units] if s else []
        due(("sum", s), place("direct", 5), call(square_sum, s, now["c"]), late)
        if s > 0:
            due(("sent", s - 1), place("handed", 2), steps[s - 1]["sent"], late + [("direct", s, 3, 0), ("direct", s, 3, 1)])
            due(("rs_sent", s - 1), place("handed", 3), steps[s - 1]["rs_sent"], late + [("direct", s, 3, 0), ("direct", s, 3, 1)])
        if s == 2:
            chain = [
                (place("direct", 5), lambda: trace_core().start()),
                (place("handed", 2), trace_core_end), (place("handed", 2), call(trace_axis_start, 1, "x")),
                (place("split_p", 3), call(trace_axis_end, 1, "x")), (place("split_p", 3), call(trace_axis_start, 2, "y")),
                (place("send_out", 5), call(trace_axis_end, 2, "y")), (place("send_out", 5), call(trace_axis_start, 3, "z")),
                (place("add_on", 7), call(trace_axis_end, 3, "z")),
            ]
            before = ("sum", 2)
            for n, (time, act) in enumerate(chain):
                due(("trace", n), time, act, [before])
                before = ("trace", n)
            due(("sent", s), place("add_on", 7), now["sent"], [("split_q", s, j) for j in units])
    for _, _, act in sorted(events.values(), key=lambda event: event[:2]):
        act()
    tr_out[...] = vsend[4]
    pat_out[...] = patf[...]
    steps[2]["rs_sent"]()
    for j in range(4):
        fin_copy(j, other).wait_recv()
    for j in range(4):
        fin_copy(j, k).wait_send()
    fin_out[...] = fin[...]


def place_body(fin, pat, totals, out, traces):
    left = lax.broadcasted_iota(jnp.int32, (128, 256), 0)
    right = lax.broadcasted_iota(jnp.int32, (128, 256), 1)
    spread = (left == right // BS).astype(F32)
    line = lax.broadcasted_iota(jnp.int32, (128, 16), 0)
    block = lax.broadcasted_iota(jnp.int32, (128, 16), 1)
    for i in range(8):
        here = [line // CH == n for n in range(4)]
        wanted = sum(jnp.where(here[n], row // BS, 0) for n, row in enumerate(lane_rows(i)))
        pick = (block == wanted).astype(F32)
        chosen = jnp.dot(pick, pat[...], preferred_element_type=F32)
        mask = jnp.dot(chosen, spread, preferred_element_type=F32)
        for half in range(2):
            lanes = slice(half * 128, (half + 1) * 128)
            part = fin[half, :, i * 128:(i + 1) * 128].T * mask[:, lanes]
            for n, row in enumerate(lane_rows(i)):
                out[row:row + CH, lanes] = part[n * CH:(n + 1) * CH]
    for i in range(STEPS):
        traces[i] = totals[i, 0]


def per_device(density, pattern, branches):
    vmem = pl.BlockSpec(memory_space=pltpu.VMEM)
    dma = pltpu.SemaphoreType.DMA
    last, totals, kept = pl.pallas_call(
        body,
        out_shape=(
            jax.ShapeDtypeStruct((2, SLAB, BLK), F32),
            jax.ShapeDtypeStruct((8, 128), F32),
            jax.ShapeDtypeStruct((16, 128), F32),
        ),
        in_specs=[vmem, vmem, pl.BlockSpec(memory_space=pltpu.SMEM)],
        out_specs=(vmem, vmem, vmem),
        scratch_shapes=[
            pltpu.VMEM((STEPS, 4, 2, SLAB, BLK), F32),
            pltpu.VMEM((STEPS, 4, SLAB, BLK), F32),
            pltpu.VMEM((2, BLK, BLK), BF16),
            pltpu.VMEM((2, BLK, BLK), BF16),
            pltpu.VMEM((4, 2 * SLAB, BLK), BF16),
            pltpu.VMEM((STEPS, 4, SLAB, BLK), F32),
            pltpu.VMEM((STEPS, 2, 4, HALF, BLK), F32),
            pltpu.VMEM((STEPS, 2, 4, CH, BLK), F32),
            pltpu.VMEM((16, 128), F32),
            pltpu.VMEM((2, 4, 16, 128), F32),
            pltpu.VMEM((2, SLAB, BLK), F32),
            pltpu.VMEM((5, 8, 128), F32),
            pltpu.VMEM((8, 128), F32),
            pltpu.VMEM((4, 4, 8, 128), F32),
            pltpu.VMEM((2, SLAB, BLK), F32),
            pltpu.VMEM((128, 128), F32),
            dma((STEPS, 2)), dma((STEPS, 2, 4)), dma((STEPS, 2, 4)),
            dma((STEPS,)), dma((STEPS, 4, 4)),
            dma((STEPS, 2)), dma((STEPS, 2, 4, 4)),
            dma((STEPS, 2)), dma((STEPS, 2, 4, 3)),
            dma((2, 4)), dma((2, 4)),
            dma((4, 4)), dma((4, 4)),
            dma((4,)), dma((4,)),
        ],
        compiler_params=pltpu.CompilerParams(
            collective_id=0, has_side_effects=True, vmem_limit_bytes=56 * 2**20
        ),
        name="purify",
    )(density, pattern.T, branches)
    smem = pl.BlockSpec(memory_space=pltpu.SMEM)
    return pl.pallas_call(
        place_body,
        out_shape=(jax.ShapeDtypeStruct((BLK, 256), F32), jax.ShapeDtypeStruct((STEPS,), F32)),
        in_specs=[vmem, vmem, smem],
        out_specs=(vmem, smem),
        name="place",
    )(last, kept, totals)


def solution(mesh):
    return jax.shard_map(
        per_device,
        mesh=mesh,
        in_specs=(P("row", "col"), P("row", "col"), P()),
        out_specs=(P("row", "col"), P()),
        check_vma=False,
    )
```

```python
import functools

import jax
import jax.numpy as jnp
from jax import lax
from jax.experimental import pallas as pl
from jax.experimental.pallas import tpu as pltpu
from jax.sharding import PartitionSpec as P

MESH = pl.DeviceIdType.MESH
STEPS = 3
BS = 64
BLK = 1024
SLAB = 128
CH = 32
HALF = 16
OFFSETS = (0, -1, 1, 2)
ORDER = {
    "ready": (
        (),
        (78, 100, 109, 112),
        (196, 199, 221, 228),
    ),
    "direct": (
        (3, 4, 6, 7, 16, 17, 27, 28),
        (106, 107, 115, 119, 129, 126, 138, 140),
        (213, 211, 215, 214, 236, 237, 244, 245),
    ),
    "handed": (
        (10, 22, 38, 39),
        (113, 131, 134, 151),
        (223, 226, 253, 259),
    ),
    "split_p": (
        (19, 30, 42, 47),
        (116, 132, 142, 158),
        (232, 242, 260, 268),
    ),
    "split_q": (
        (50, 64, 83, 85),
        (147, 166, 186, 204),
        (250, 273, 292, 305),
    ),
    "product": (
        (51, 53, 54, 55, 65, 66, 67, 71, 92, 93, 94, 95, 86, 87, 88, 89),
        (148, 149, 150, 159, 167, 168, 169, 170, 187, 188, 189, 190, 205, 206, 207, 208),
        (251, 252, 261, 269, 276, 277, 280, 282, 293, 295, 299, 300, 306, 307, 308, 309),
    ),
    "send_out": (
        (56, 57, 72, 73, 96, 97, 91, 90),
        (160, 161, 172, 177, 191, 192, 209, 210),
        (270, 271, 283, 284, 301, 302, 310, 311),
    ),
    "add_on": (
        (68, 69, 79, 80, 103, 102, 104, 105),
        (178, 180, 182, 183, 201, 202, 217, 218),
        (288, 287, 296, 298, 313, 312, 315, 316),
    ),
    "end": (
        (77, 99, 108, 111),
        (195, 198, 220, 227),
        (314, 317, 318, 319),
    ),
    "bc": (
        (0, 2, 15, 5, 11, 25, 8, 20, 33, 23, 40, 49, 1, 9, 18, 13, 26, 37, 14, 29, 41, 35, 52, 63, 12, 24, 34, 31, 44, 82, 32, 48, 60, 58, 70, 81, 21, 36, 46, 43, 61, 75, 45, 62, 76, 59, 74, 84),
        (98, 101, 118, 114, 123, 135, 117, 128, 136, 120, 130, 143, 110, 121, 124, 122, 133, 146, 125, 141, 154, 139, 153, 165, 127, 145, 157, 144, 162, 175, 152, 171, 181, 155, 174, 184, 137, 156, 176, 163, 179, 194, 164, 193, 197, 173, 185, 203),
        (200, 212, 225, 219, 230, 240, 224, 234, 241, 229, 239, 249, 216, 222, 233, 231, 243, 256, 235, 248, 264, 246, 258, 272, 238, 254, 267, 255, 266, 285, 257, 275, 290, 263, 281, 291, 247, 262, 279, 265, 286, 297, 274, 289, 303, 278, 294, 304),
    ),
}
ROLES = (("x", "z", "y"), ("z", "y", "x"), ("y", "x", "z"))
F32 = jnp.float32
BF16 = jnp.bfloat16


def nt_dot(left, right):
    return lax.dot_general(left, right, (((1,), (1,)), ((), ())), preferred_element_type=F32)


def split(value):
    high = value.astype(BF16)
    return high, (value - high.astype(F32)).astype(BF16)


def lane_rows(i):
    unit = i // 2
    return [(2 * (i % 2) + q) * 256 + core * SLAB + unit * CH for q in (0, 1) for core in (0, 1)]


def body(
    dens, pat, br, fin_out, tr_out, pat_out,
    pbuf, qbuf, phi, plo, qcat, obuf, r1, r2, patf, gbuf, mbuf, vsend, vcore, vaxis, fin, wide,
    ag_s, ag_r, af_r, cx_s, cx_r, bc_s, bc_r, rs_s, rs_r, pt_s, pt_r, tr_s, tr_r, fx_s, fx_r,
):
    col = lax.axis_index("col")
    k = lax.axis_index("depth")
    pos = {"x": lax.axis_index("row"), "y": lax.rem(col, 4), "z": lax.div(col, 4)}
    other = 1 - k

    def wrap(value):
        return lax.rem(value + 8, 4)

    def device(x, y, z, core):
        return (x, z * 4 + y, core)

    def at(axis, delta):
        place = dict(pos)
        place[axis] = wrap(place[axis] + delta)
        return device(place["x"], place["y"], place["z"], k)

    partner = device(pos["x"], pos["y"], pos["z"], other)

    def rcopy(src, dst, send, recv, dev):
        return pltpu.make_async_remote_copy(
            src_ref=src, dst_ref=dst, send_sem=send, recv_sem=recv, device_id=dev, device_id_type=MESH
        )

    barrier = pltpu.get_barrier_semaphore()
    greet = [partner]
    for axis in ("x", "y", "z"):
        for delta in (1, -1, 2):
            greet.append(at(axis, delta))
    for i in range(4):
        greet.append(device(pos["y"], i, pos["z"], other))
        greet.append(device(pos["x"], i, pos["y"], other))
    for dev in greet:
        pl.semaphore_signal(barrier, inc=1, device_id=dev, device_id_type=MESH)

    for i in range(8):
        mine = pl.ds(pl.multiple_of(k * 128, 128), 128)
        piece = jnp.concatenate([dens[row:row + CH, mine] for row in lane_rows(i)], axis=0)
        pbuf[0, pos["y"], k, :, i * 128:(i + 1) * 128] = piece.T
    vsend[0] = jnp.zeros((8, 128), F32)
    wide[...] = jnp.zeros_like(wide)
    wide[0:4, 0:16] = pat[...].astype(F32)
    patf[...] = wide[...].T[0:16, :]
    pl.semaphore_wait(barrier, len(greet))

    def pattern_copies():
        found = []
        for i in range(4):
            found.append(rcopy(patf, gbuf.at[0, pos["y"]], pt_s.at[0, i], pt_r.at[0, pos["y"]],
                               device(i, pos["x"], pos["z"], other)))
            found.append(rcopy(patf, gbuf.at[1, pos["y"]], pt_s.at[1, i], pt_r.at[1, pos["y"]],
                               device(pos["x"], pos["z"], i, other)))
        return found

    def pattern_wait(s):
        for i in range(4):
            rcopy(patf, gbuf.at[s, i], pt_s.at[s, i], pt_r.at[s, i], partner).wait_recv()

    def square_sum(s, slab):
        total = jnp.zeros((1, BLK), F32)
        for i in range(4):
            part = pbuf[s, slab, k, i * CH:(i + 1) * CH, :]
            total = total + jnp.sum(part * part, axis=0, keepdims=True)
        vsend[0, s:s + 1, :] = jnp.broadcast_to(jnp.sum(total, axis=1, keepdims=True), (1, 128))

    def trace_core():
        return rcopy(vsend.at[0], vcore, tr_s.at[0, 0], tr_r.at[0, 0], partner)

    def trace_core_end():
        trace_core().wait()
        vsend[1] = vsend[0] + vcore[...]

    def trace_axis_copies(stage, axis):
        me = pos[axis]
        return [
            rcopy(vsend.at[stage], vaxis.at[stage, me], tr_s.at[stage, d], tr_r.at[stage, me], at(axis, d))
            for d in (1, 2, 3)
        ]

    def trace_axis_start(stage, axis):
        for copy in trace_axis_copies(stage, axis):
            copy.start()
        vaxis[stage, pos[axis]] = vsend[stage]

    def trace_axis_end(stage, axis):
        for d in (1, 2, 3):
            src = wrap(pos[axis] + d)
            rcopy(vsend.at[stage], vaxis.at[stage, src], tr_s.at[stage, d], tr_r.at[stage, src], partner).wait_recv()
        for copy in trace_axis_copies(stage, axis):
            copy.wait_send()
        vsend[stage + 1] = (vaxis[stage, 0] + vaxis[stage, 1]) + (vaxis[stage, 2] + vaxis[stage, 3])

    def fin_copy(j, core):
        ref = fin.at[core, pl.ds(j * CH, CH)]
        return rcopy(ref, ref, fx_s.at[j], fx_r.at[j], partner)

    def make_step(s):
        step = {}
        an, bn, cn = ROLES[s]
        a, b, c = pos[an], pos[bn], pos[cn]
        d = wrap(b - c)
        root = d == 0
        up, down, far = wrap(a + 1), wrap(a - 1), wrap(a + 2)

        def rows(j):
            return pl.ds(j * CH, CH)

        def half_rows(j, direction):
            return pl.ds(j * CH + direction * HALF, HALF)

        def sign(direction):
            return 1 - 2 * direction

        def ag_copy(direction, j):
            ref = pbuf.at[s, c, k, rows(j)]
            return rcopy(ref, ref, ag_s.at[s, direction], ag_r.at[s, direction, j], at(cn, sign(direction)))

        def ag_wait(direction, j):
            ref = pbuf.at[s, wrap(c - sign(direction)), k, rows(j)]
            rcopy(ref, ref, ag_s.at[s, direction], ag_r.at[s, direction, j], partner).wait_recv()

        def af_copy(direction, j):
            ref = pbuf.at[s, wrap(c - sign(direction)), k, half_rows(j, direction)]
            return rcopy(ref, ref, ag_s.at[s, direction], af_r.at[s, direction, j], at(cn, sign(direction)))

        def af_wait(direction, j):
            ref = pbuf.at[s, wrap(c + 2), k, half_rows(j, direction)]
            rcopy(ref, ref, ag_s.at[s, direction], af_r.at[s, direction, j], partner).wait_recv()

        def cx_copy(j, i):
            ref = pbuf.at[s, wrap(c + OFFSETS[i]), k, rows(j)]
            return rcopy(ref, ref, cx_s.at[s], cx_r.at[s, j, i], partner)

        def cx_wait(j, i):
            ref = pbuf.at[s, wrap(c + OFFSETS[i]), other, rows(j)]
            rcopy(ref, ref, cx_s.at[s], cx_r.at[s, j, i], partner).wait_recv()

        def bc_copy(direction, j, i, from_root):
            q = wrap(c + OFFSETS[i])
            place = half_rows(j, direction)
            dst = qbuf.at[s, q, place]
            src = pbuf.at[s, q, k, place] if from_root else dst
            return rcopy(src, dst, bc_s.at[s, direction], bc_r.at[s, direction, j, i], at(bn, sign(direction)))

        def bc_root(j, *parts):
            @pl.when(root)
            def _():
                for i in parts:
                    bc_copy(0, j, i, True).start()
                    bc_copy(1, j, i, True).start()

        def bc_hop(hop, j, i):
            def hand_on(*directions):
                for direction in directions:
                    copy = bc_copy(direction, j, i, False)
                    copy.wait_recv()
                    if hop < 3:
                        copy.start()

            if hop == 2:
                pl.when(d == 2)(functools.partial(hand_on, 0, 1))
            else:
                pl.when(d == hop)(functools.partial(hand_on, 0))
                pl.when(d == 4 - hop)(functools.partial(hand_on, 1))

        def ready(j):
            ag_copy(0, j).start()
            ag_copy(1, j).start()
            bc_root(j, 0)
            cx_copy(j, 0).start()

        def direct(j, direction):
            ag_wait(direction, j)
            af_copy(direction, j).start()
            if s == 0 and j < 2 and direction == 1:
                ready(j + 2)
            cx_copy(j, 1 + direction).start()
            bc_root(j, 1 + direction)

        def handed(j):
            for direction in (0, 1):
                af_wait(direction, j)
            cx_copy(j, 3).start()
            bc_root(j, 3)

        def split_p(j):
            for i in range(4):
                cx_wait(j, i)

            @pl.loop(0, 8)
            def _(i):
                row = pl.multiple_of(j * 8 * CH + i * CH, CH)
                high, low = split(pbuf[s, lax.div(i, 2), lax.rem(i, 2), rows(j)])
                phi[s % 2, pl.ds(row, CH), :] = high
                plo[s % 2, pl.ds(row, CH), :] = low

        def split_q(j):
            def halves(read):
                for q in range(4):
                    high, low = split(read(q))
                    qcat[j, q * CH:(q + 1) * CH, :] = high
                    qcat[j, SLAB + q * CH:SLAB + (q + 1) * CH, :] = low

            @pl.when(root)
            def _():
                halves(lambda q: pbuf[s, q, k, rows(j)])

            @pl.when(jnp.logical_not(root))
            def _():
                halves(lambda q: qbuf[s, q, rows(j)])

        def product(j, first, last):
            weight = br[s].astype(F32)
            scale = 1.0 - 2.0 * weight
            linear = 2.0 * weight * (a == b).astype(F32)

            @pl.loop(first, last)
            def _(n):
                lanes = pl.ds(pl.multiple_of(n * 256, 256), 256)
                both = nt_dot(qcat[j], phi[s % 2, lanes, :])
                value = both[:SLAB] + both[SLAB:] + nt_dot(qcat[j, :SLAB, :], plo[s % 2, lanes, :])
                same = qcat[j, :SLAB, lanes].astype(F32) + qcat[j, SLAB:, lanes].astype(F32)
                obuf[s, j, :, lanes] = scale * value + linear * same

        def send_out(j, i):
            for direction in (0, 1):
                rs_copy(direction, i, j).start()

        def out_half(q, second):
            return pl.ds(pl.multiple_of(q * CH + second * HALF, HALF), HALF)

        def rs_copy(direction, i, j):
            near = up if direction == 0 else down
            if i == 0:
                src, dst = obuf.at[s, j, out_half(far, direction)], r1.at[s, direction, j]
            else:
                second = 1 - direction if i == 1 else direction
                src = obuf.at[s, j, out_half(near, second)]
                dst = r2.at[s, direction, j, pl.ds(second * HALF, HALF)]
            return rcopy(src, dst, rs_s.at[s, direction], rs_r.at[s, direction, j, i], at(an, sign(direction)))

        def add_on(j, direction):
            rs_copy(direction, 0, j).wait_recv()
            place = out_half(up if direction == 0 else down, direction)
            obuf[s, j, place, :] = obuf[s, j, place, :] + r1[s, direction, j]
            rs_copy(direction, 2, j).start()

        def mask():
            pattern_wait(s)
            line = lax.broadcasted_iota(jnp.int32, (SLAB, 16), 0)
            block = lax.broadcasted_iota(jnp.int32, (SLAB, 16), 1)
            pick = (block == a * 4 + k * 2 + line // BS).astype(F32)
            left = lax.broadcasted_iota(jnp.int32, (128, 256), 0)
            right = lax.broadcasted_iota(jnp.int32, (128, 256), 1)
            chosen = [jnp.dot(pick, gbuf[s, q], preferred_element_type=F32) for q in range(4)]
            for pair in range(2):
                value = jnp.zeros((SLAB, 256), F32)
                for q in range(4):
                    wanted = (right % 64) // CH * 2 + pair
                    spread = jnp.logical_and(right // 64 == q, left == wanted).astype(F32)
                    value = value + jnp.dot(chosen[q], spread, preferred_element_type=F32)
                for i in (2 * pair, 2 * pair + 1):
                    mbuf[s, :, i * 256:(i + 1) * 256] = value

        def finish(j):
            for i in (1, 2):
                for direction in (0, 1):
                    rs_copy(direction, i, j).wait_recv()
            place = pl.ds(pl.multiple_of(a * CH, CH), CH)
            value = obuf[s, j, place, :] + (r2[s, 0, j] + r2[s, 1, j])
            if s < 2:
                pbuf[s + 1, a, k, rows(j), :] = value * mbuf[s, rows(j), :]
            else:
                fin[k, rows(j), :] = value
                fin_copy(j, k).start()

        def all_sent(ref, send, recv):
            rcopy(ref, ref, send, recv, partner).wait_send()

        def sent():
            for direction in (0, 1):
                all_sent(pbuf.at[s, 0, :, pl.ds(0, 96)], ag_s.at[s, direction], ag_r.at[s, direction, 0])

                @pl.when(d != (3 if direction == 0 else 1))
                def _():
                    all_sent(qbuf.at[s, pl.ds(0, 2)], bc_s.at[s, direction], bc_r.at[s, direction, 0, 0])
            all_sent(qbuf.at[s], cx_s.at[s], cx_r.at[s, 0, 0])
            if s == 0:
                for copy in pattern_copies():
                    copy.wait_send()

        def rs_sent():
            for direction in (0, 1):
                all_sent(obuf.at[s, pl.ds(0, 2), pl.ds(0, 96)], rs_s.at[s, direction], rs_r.at[s, direction, 0, 0])

        step.update(locals())
        return step

    steps = [make_step(s) for s in range(STEPS)]
    steps[0]["ready"](0)
    steps[0]["ready"](1)
    for copy in pattern_copies():
        copy.start()

    events = {}

    def due(name, time, act, needs=()):
        time = max([time] + [events[need][0] for need in needs])
        events[name] = (time, len(events), act)

    call = functools.partial
    units = range(4)
    hops = (1, 2, 3)
    for s in range(STEPS):
        now = steps[s]

        def place(kind, n):
            return ORDER[kind][s][n]

        for j in units:
            begun = [("direct", 0, j - 2, 1)] if j > 1 else []
            if s:
                due(("ready", s, j), place("ready", j), call(now["ready"], j), [("end", s - 1, j)])
                begun = [("ready", s, j)]
            for n in (0, 1):
                due(("direct", s, j, n), place("direct", 2 * j + n), call(now["direct"], j, n), begun)
            due(("handed", s, j), place("handed", j), call(now["handed"], j), [("direct", s, j, 0), ("direct", s, j, 1)])
            due(("split_p", s, j), place("split_p", j), call(now["split_p"], j), [("handed", s, j)])
            starts = (begun, [("direct", s, j, 0)], [("direct", s, j, 1)], [("handed", s, j)])
            for i in units:
                for hop in hops:
                    needs = [("bc", s, j, i, hop - 1)] if hop > 1 else starts[i]
                    due(("bc", s, j, i, hop), place("bc", j * 12 + i * 3 + hop - 1), call(now["bc_hop"], hop, j, i), needs)
        if s < 2:
            due(("mask", s), ORDER["direct"][0][2 + 2 * s], now["mask"])
        for j in units:
            due(("split_q", s, j), place("split_q", j), call(now["split_q"], j),
                [("bc", s, j, i, hop) for i in units for hop in hops] + [("handed", s, j)])
            before = ("split_q", s, j)
            for n in units:
                due(("product", s, j, n), place("product", j * 4 + n), call(now["product"], j, n, n + 1),
                    [before, ("split_p", s, n)])
                before = ("product", s, j, n)
            for n in (0, 1):
                due(("send_out", s, j, n), place("send_out", 2 * j + n), call(now["send_out"], j, n), [before])
            for n in (0, 1):
                due(("add_on", s, j, n), place("add_on", 2 * j + n), call(now["add_on"], j, n), [("send_out", s, j, 0)])
            due(("end", s, j), place("end", j), call(now["finish"], j),
                [("add_on", s, j, 0), ("add_on", s, j, 1), ("send_out", s, j, 1)] + ([("mask", s)] if s < 2 else []))
        late = [("end", s - 1, n) for n in units] if s else []
        due(("sum", s), place("direct", 5), call(square_sum, s, now["c"]), late)
        if s > 0:
            due(("sent", s - 1), place("handed", 2), steps[s - 1]["sent"], late + [("direct", s, 3, 0), ("direct", s, 3, 1)])
            due(("rs_sent", s - 1), place("handed", 3), steps[s - 1]["rs_sent"], late + [("direct", s, 3, 0), ("direct", s, 3, 1)])
        if s == 2:
            chain = [
                (place("direct", 5), lambda: trace_core().start()),
                (place("handed", 2), trace_core_end), (place("handed", 2), call(trace_axis_start, 1, "x")),
                (place("split_p", 3), call(trace_axis_end, 1, "x")), (place("split_p", 3), call(trace_axis_start, 2, "y")),
                (place("send_out", 5), call(trace_axis_end, 2, "y")), (place("send_out", 5), call(trace_axis_start, 3, "z")),
                (place("add_on", 7), call(trace_axis_end, 3, "z")),
            ]
            before = ("sum", 2)
            for n, (time, act) in enumerate(chain):
                due(("trace", n), time, act, [before])
                before = ("trace", n)
            due(("sent", s), place("add_on", 7), now["sent"], [("split_q", s, j) for j in units])
    for _, _, act in sorted(events.values(), key=lambda event: event[:2]):
        act()
    tr_out[...] = vsend[4]
    pat_out[...] = patf[...]
    steps[2]["rs_sent"]()
    for j in range(4):
        fin_copy(j, other).wait_recv()
    for j in range(4):
        fin_copy(j, k).wait_send()
    fin_out[...] = fin[...]


def place_body(fin, pat, totals, out, traces):
    left = lax.broadcasted_iota(jnp.int32, (128, 256), 0)
    right = lax.broadcasted_iota(jnp.int32, (128, 256), 1)
    spread = (left == right // BS).astype(F32)
    line = lax.broadcasted_iota(jnp.int32, (128, 16), 0)
    block = lax.broadcasted_iota(jnp.int32, (128, 16), 1)
    for i in range(8):
        here = [line // CH == n for n in range(4)]
        wanted = sum(jnp.where(here[n], row // BS, 0) for n, row in enumerate(lane_rows(i)))
        pick = (block == wanted).astype(F32)
        chosen = jnp.dot(pick, pat[...], preferred_element_type=F32)
        mask = jnp.dot(chosen, spread, preferred_element_type=F32)
        for half in range(2):
            lanes = slice(half * 128, (half + 1) * 128)
            part = fin[half, :, i * 128:(i + 1) * 128].T * mask[:, lanes]
            for n, row in enumerate(lane_rows(i)):
                out[row:row + CH, lanes] = part[n * CH:(n + 1) * CH]
    for i in range(STEPS):
        traces[i] = totals[i, 0]


def per_device(density, pattern, branches):
    vmem = pl.BlockSpec(memory_space=pltpu.VMEM)
    dma = pltpu.SemaphoreType.DMA
    last, totals, kept = pl.pallas_call(
        body,
        out_shape=(
            jax.ShapeDtypeStruct((2, SLAB, BLK), F32),
            jax.ShapeDtypeStruct((8, 128), F32),
            jax.ShapeDtypeStruct((16, 128), F32),
        ),
        in_specs=[vmem, vmem, pl.BlockSpec(memory_space=pltpu.SMEM)],
        out_specs=(vmem, vmem, vmem),
        scratch_shapes=[
            pltpu.VMEM((STEPS, 4, 2, SLAB, BLK), F32),
            pltpu.VMEM((STEPS, 4, SLAB, BLK), F32),
            pltpu.VMEM((2, BLK, BLK), BF16),
            pltpu.VMEM((2, BLK, BLK), BF16),
            pltpu.VMEM((4, 2 * SLAB, BLK), BF16),
            pltpu.VMEM((STEPS, 4, SLAB, BLK), F32),
            pltpu.VMEM((STEPS, 2, 4, HALF, BLK), F32),
            pltpu.VMEM((STEPS, 2, 4, CH, BLK), F32),
            pltpu.VMEM((16, 128), F32),
            pltpu.VMEM((2, 4, 16, 128), F32),
            pltpu.VMEM((2, SLAB, BLK), F32),
            pltpu.VMEM((5, 8, 128), F32),
            pltpu.VMEM((8, 128), F32),
            pltpu.VMEM((4, 4, 8, 128), F32),
            pltpu.VMEM((2, SLAB, BLK), F32),
            pltpu.VMEM((128, 128), F32),
            dma((STEPS, 2)), dma((STEPS, 2, 4)), dma((STEPS, 2, 4)),
            dma((STEPS,)), dma((STEPS, 4, 4)),
            dma((STEPS, 2)), dma((STEPS, 2, 4, 4)),
            dma((STEPS, 2)), dma((STEPS, 2, 4, 3)),
            dma((2, 4)), dma((2, 4)),
            dma((4, 4)), dma((4, 4)),
            dma((4,)), dma((4,)),
        ],
        compiler_params=pltpu.CompilerParams(
            collective_id=0, has_side_effects=True, vmem_limit_bytes=56 * 2**20
        ),
        name="purify",
    )(density, pattern.T, branches)
    smem = pl.BlockSpec(memory_space=pltpu.SMEM)
    return pl.pallas_call(
        place_body,
        out_shape=(jax.ShapeDtypeStruct((BLK, 256), F32), jax.ShapeDtypeStruct((STEPS,), F32)),
        in_specs=[vmem, vmem, smem],
        out_specs=(vmem, smem),
        name="place",
    )(last, kept, totals)


def solution(mesh):
    return jax.shard_map(
        per_device,
        mesh=mesh,
        in_specs=(P("row", "col"), P("row", "col"), P()),
        out_specs=(P("row", "col"), P()),
        check_vma=False,
    )
```
